32 devices in a mesh: req: 16 (over z, y, x), head: 2 (over core).
Axes of the slice: x: 2, y: 2, z: 4, core: 2. Of those that a mesh axis runs over, the one named last changes fastest.
Arguments:
- verify_x: bfloat16 [16, 5, 2048], P('req'), may hold values from -6 to 6
- prefill_x: bfloat16 [4096, 2048], P('req'), may hold values from -6 to 6
- attn_gain: float32 [2048], replicated, may hold values from 0.25 to 1.75
- w_query: bfloat16 [2048, 2048], P(None, 'head'), may hold values from -0.125 to 0.125
- w_keyval: bfloat16 [2048, 1024], P(None, 'head'), may hold values from -0.125 to 0.125
- qk_gain: float32 [2, 256], replicated, may hold values from 0.25 to 8
- w_out: bfloat16 [2048, 2048], P('head'), may hold values from -0.125 to 0.125
- post_gain: float32 [2048], replicated, may hold values from 0.1 to 1.9
- page_pool: bfloat16 [1024, 16, 1024], P('req', None, 'head'), may hold values from -6 to 6
- outbound: int32 [16, 16], P('req'), may hold values from -1 to 63, as said below
- page_table: int32 [16, 64], P('req'), may hold values from 0 to 79, as said below
- cache_len: int32 [16], P('req'), may hold values from 1 to 1024, as said below
- prompt_len: int32 [16, 4], P('req'), may hold values from 1 to 128, 256 in all within a row
- accepted: int32 [16], P('req'), may hold values from 0 to 5
Outputs:
- verify_out: bfloat16 [16, 5, 2048], P('req', None, 'head')
- prefill_out: bfloat16 [4096, 2048], P('req', 'head')
- verify_kv: bfloat16 [16, 5, 1024], P('req', None, 'head')
- prefill_kv: bfloat16 [4096, 1024], P('req', 'head')
The draws below stay inside these ranges and needn't reach their ends.
Inputs may be any that keep to these rules, and one draw needn't show every extreme that they name: `outbound`: row s names a page of device s's pool for every device d other than s; the entry at d = s is -1. `page_table`: an entry below 64 names a page of the device's own pool; an entry 64 + s names the page received from device s, s never the device itself. `cache_len`: some request has exactly 1024 cached tokens.
All inputs are finite; a program needn't handle non-finite values.
Results may differ from the reference program's by a relative error of at most 0.015.
The reference program's roundings to bfloat16 on the way count: a program that leaves them out, or rounds other values in their place, can miss the bound.
Values may be sent and summed in bfloat16 or wider, within the bound.
A program may use at most 64 MiB of HBM per device.

```python
import math
import jax
import jax.numpy as jnp
import numpy as np
from jax import lax

D = 2048
HEADS = 8
KV_HEADS = 2
HEAD = 256
DRAFT = 5
PAGE = 16
CACHE = 1024
MAXP = 64
REQ_DEV = 1
POOL_DEV = 64
REQS = 16
PREF_DEV = 256
PROMPTS = 4
PREFILL = 4096
N_REQ = 16


def migration_plan(key):
    key_page = jax.random.fold_in(jax.random.fold_in(key, 7), 1)
    send_plan = jax.random.randint(key_page, (N_REQ, N_REQ), 0, POOL_DEV)
    send_plan = send_plan.at[1, 0].set(POOL_DEV - 1)
    send_plan = send_plan.at[N_REQ - 1, 0].set(0)
    on_diagonal = jnp.arange(N_REQ, dtype=jnp.int32)[:, None] == jnp.arange(N_REQ, dtype=jnp.int32)[None, :]
    send_plan = jnp.where(on_diagonal, -1, send_plan)
    return send_plan.astype(jnp.int32)


def draw_outbound(key, part):
    return migration_plan(key)


def draw_page_table(key, part):
    send_plan = migration_plan(key)
    candidate = jax.random.randint(jax.random.fold_in(key, 11), (REQS, MAXP), 0, POOL_DEV + N_REQ)
    device = (jnp.arange(REQS, dtype=jnp.int32) // REQ_DEV)[:, None]
    source = jnp.clip(candidate - POOL_DEV, 0, N_REQ - 1)
    arrived = send_plan[source, device] >= 0
    valid = (candidate < POOL_DEV) | arrived
    page_list = jnp.where(valid, candidate, candidate % POOL_DEV)
    page_list = page_list.at[0, 0].set(POOL_DEV + N_REQ - 1)
    return page_list.astype(jnp.int32)


def draw_cache_len(key, part):
    lengths = jax.random.randint(jax.random.fold_in(key, 13), (REQS,), 1, CACHE + 1)
    return lengths.at[0].set(CACHE).astype(jnp.int32)


def draw_qk_gain(key, part):
    key_base = jax.random.fold_in(jax.random.fold_in(key, 17), 0)
    gains = 1.0 + 0.15 * jnp.clip(jax.random.normal(key_base, (2, HEAD), jnp.float32), -5.0, 5.0)
    return gains


def draw_page_pool(key, part):
    shape = (N_REQ * POOL_DEV, PAGE, KV_HEADS * 2 * HEAD)
    key_body = jax.random.fold_in(jax.random.fold_in(key, 19), 0)
    entries = jnp.clip(jax.random.normal(key_body, shape, jnp.float32), -6.0, 6.0)
    return entries.astype(jnp.bfloat16)


def place_ends(values, own_key, low, top_value):
    shape = values.shape
    spot = [jax.random.randint(jax.random.fold_in(own_key, axis), (), 0, shape[axis]) for axis in range(len(shape))]
    values = values.at[tuple(spot)].set(low)
    longest = shape.index(max(shape))
    spot[longest] = (spot[longest] + 1) % shape[longest]
    return values.at[tuple(spot)].set(top_value)


def shard_levels(rng, extent, cuts, least, high):
    loudness = 1.0
    for dim, parts in cuts:
        draws = jax.random.uniform(jax.random.fold_in(jax.random.fold_in(rng, 6), dim), (parts,), jnp.float32, least / len(cuts), high / len(cuts))
        loudness = loudness * jnp.repeat(jnp.exp(draws), extent[dim] // parts).reshape((-1,) + (1,) * (len(extent) - 1 - dim))
    return loudness


def length_profile(number_of, total, most, slope):
    loads = [(1 << 20) // math.isqrt(rank ** slope) + 1 for rank in range(2, number_of + 1)]
    rest, counts = total - most - (number_of - 1), [1] * (number_of - 1)
    while rest > 0:
        candidates = [i for i in range(number_of - 1) if counts[i] < most]
        mass, left = sum([loads[i] for i in candidates]), rest
        for i in candidates:
            addition = min(most - counts[i], max(1, left * loads[i] // mass), rest)
            counts[i] = counts[i] + addition
            rest = rest - addition
    return np.array([most] + counts)


def ragged_sizes(rng, number_of, total, limit, lean):
    if number_of == 2:
        one = jax.random.randint(rng, (), max(1, total - limit), min(limit, total - 1) + 1)
        return jnp.stack([one, total - one])
    sizes = jnp.asarray(length_profile(number_of, total, limit, lean), jnp.int32)
    pairs = (number_of - 1) // 2
    donor, receiver = sizes[1:1 + 2 * pairs:2], sizes[2:2 + 2 * pairs:2]
    margin = jnp.minimum(donor - 1, limit - receiver)
    moved = jax.random.randint(jax.random.fold_in(rng, 1), (pairs,), 0, 1 << 20) % (margin + 1)
    sizes = sizes.at[1:1 + 2 * pairs:2].set(donor - moved).at[2:2 + 2 * pairs:2].set(receiver + moved)
    return sizes[jax.random.permutation(jax.random.fold_in(rng, 2), number_of)]


def scatter_about(own_key, extent, deviation, most, cuts=(), kind=jnp.bfloat16):
    drawn = jax.random.normal(own_key, extent, jnp.float32) * deviation
    if len(cuts) > 0:
        drawn = shard_levels(own_key, extent, cuts, -0.22, 0.18) * drawn
    return jnp.clip(drawn, min=-most, max=most).astype(kind)


def setup_inputs(seed: int = 0) -> dict:
    key_list = jax.random.split(jax.random.key(seed), 15)
    return {
        "verify_x": scatter_about(key_list[0], (REQS, DRAFT, D), 1.0, 6.0, ((0, 16),)),
        "prefill_x": scatter_about(key_list[1], (PREFILL, D), 1.0, 6.0, ((0, 16),)),
        "attn_gain": jnp.clip(1.0 + 0.15 * jax.random.normal(key_list[2], (D,), jnp.float32), 0.25, 1.75),
        "w_query": scatter_about(key_list[3], (D, HEADS * HEAD), D ** -0.5, 0.125, ((1, 2),)),
        "w_keyval": scatter_about(key_list[4], (D, KV_HEADS * 2 * HEAD), D ** -0.5, 0.125, ((1, 2),)),
        "qk_gain": draw_qk_gain(jax.random.fold_in(key_list[14], 71), 0),
        "w_out": scatter_about(key_list[6], (HEADS * HEAD, D), (HEADS * HEAD) ** -0.5, 0.125, ((0, 2),)),
        "post_gain": jnp.clip(1.0 + 0.18 * jax.random.normal(key_list[7], (D,), jnp.float32), 0.1, 1.9),
        "page_pool": draw_page_pool(jax.random.fold_in(key_list[14], 71), 0),
        "outbound": draw_outbound(jax.random.fold_in(key_list[14], 71), 0),
        "page_table": draw_page_table(jax.random.fold_in(key_list[14], 71), 0),
        "cache_len": draw_cache_len(jax.random.fold_in(key_list[14], 71), 0),
        "prompt_len": jax.vmap(lambda own: ragged_sizes(own, PROMPTS, PREF_DEV, PREF_DEV // 2, 2))(jax.random.split(key_list[12], N_REQ)).reshape((N_REQ, PROMPTS)).astype(jnp.int32),
        "accepted": place_ends(jax.random.randint(key_list[13], (REQS,), 0, DRAFT + 1), jax.random.fold_in(key_list[13], 1), 0, DRAFT).astype(jnp.int32),
    }


eps_norm = 1e-06
rope_base = 1000000.0
neg_large = -1e+30

def rms_scale(values):
    return values * lax.rsqrt(lax.optimization_barrier(jnp.mean(values * values, axis=-1, keepdims=True)) + eps_norm)

def rotate(values, position):
    half_dim = values.shape[-1] // 2
    inv_freq = rope_base ** (-(jnp.arange(half_dim, dtype=jnp.float32) * 2.0) / values.shape[-1])
    angles = position[:, None, None] * inv_freq[None, None, :]
    cosine = jnp.cos(angles)
    sine_part = jnp.sin(angles)
    first = values[..., :half_dim]
    second = values[..., half_dim:]
    return jnp.concatenate([first * cosine - second * sine_part, second * cosine + first * sine_part], axis=-1)

def project(hidden_rows, attn_gain, w_query, w_keyval, qk_gain, position):
    row_count = hidden_rows.shape[0]
    normed = (rms_scale(hidden_rows.astype(jnp.float32)) * attn_gain).astype(jnp.bfloat16)
    query_rows = jnp.dot(normed, w_query, preferred_element_type=jnp.float32).reshape(row_count, -1, HEAD)
    query_rows = rotate(rms_scale(query_rows) * qk_gain[0], position).astype(jnp.bfloat16)
    keyval = jnp.dot(normed, w_keyval, preferred_element_type=jnp.float32).reshape(row_count, -1, 2, HEAD)
    key_rows = rotate(rms_scale(keyval[:, :, 0]) * qk_gain[1], position).astype(jnp.bfloat16)
    value_rows = rms_scale(keyval[:, :, 1]).astype(jnp.bfloat16)
    return (query_rows, key_rows, value_rows)

def attend(query_rows, key_rows, value_rows, allowed):
    row_count = query_rows.shape[0]
    groups = key_rows.shape[1]
    grouped = query_rows.reshape(row_count, groups, -1, HEAD).astype(jnp.float32)
    scores = jnp.einsum('tgqe,jge->gqtj', grouped, key_rows.astype(jnp.float32))
    scores = jnp.where(allowed[None, None], scores, neg_large)
    peak_score = lax.optimization_barrier(jnp.max(scores, axis=-1, keepdims=True))
    weights = jnp.exp(scores - peak_score)
    denom_sum = lax.optimization_barrier(jnp.sum(weights, axis=-1, keepdims=True))
    attn_probs = (weights / denom_sum).astype(jnp.bfloat16)
    mixed_heads = jnp.einsum('gqtj,jge->tgqe', attn_probs.astype(jnp.float32), value_rows.astype(jnp.float32))
    return mixed_heads.reshape(row_count, -1).astype(jnp.bfloat16)

def prompt_layout(lengths, row_count):
    prompt_ends = jnp.cumsum(lengths)
    row_index = jnp.arange(row_count, dtype=jnp.int32)
    segment = lax.optimization_barrier(jnp.sum((row_index[:, None] >= prompt_ends[None, :]).astype(jnp.int32), axis=1))
    starts = prompt_ends - lengths
    which = segment[:, None] == jnp.arange(lengths.shape[0], dtype=jnp.int32)[None, :]
    start_row = lax.optimization_barrier(jnp.sum(jnp.where(which, starts[None, :], 0), axis=1))
    position = (row_index - start_row).astype(jnp.float32)
    allowed = (segment[:, None] == segment[None, :]) & (row_index[None, :] <= row_index[:, None])
    return (position, allowed)

def reference(verify_x, prefill_x, attn_gain, w_query, w_keyval, qk_gain, w_out, post_gain, page_pool, outbound, page_table, cache_len, prompt_len, accepted):
    groups = KV_HEADS

    def one_request(request):
        device = request // REQ_DEV
        position = (cache_len[request] + jnp.arange(DRAFT, dtype=jnp.int32)).astype(jnp.float32)
        query_rows, key_rows, value_rows = project(verify_x[request], attn_gain, w_query, w_keyval, qk_gain, position)
        page_list = page_table[request]
        source = jnp.clip(page_list - POOL_DEV, 0, N_REQ - 1).astype(jnp.int32)
        sent_page = outbound[source, device]
        is_local = page_list < POOL_DEV
        flat_index = jnp.where(is_local, device * POOL_DEV + page_list, source * POOL_DEV + jnp.clip(sent_page, 0, POOL_DEV - 1)).astype(jnp.int32)
        is_live = is_local | (sent_page >= 0)
        page_rows = jnp.take(page_pool, flat_index, axis=0)
        page_rows = jnp.where(is_live[:, None, None], page_rows, jnp.zeros_like(page_rows))
        cached = page_rows.reshape(CACHE, groups, 2, HEAD)
        all_keys = jnp.concatenate([cached[:, :, 0], key_rows], axis=0)
        all_values = jnp.concatenate([cached[:, :, 1], value_rows], axis=0)
        slot = jnp.arange(CACHE + DRAFT, dtype=jnp.int32)
        step_index = jnp.arange(DRAFT, dtype=jnp.int32)
        allowed = jnp.where(slot[None, :] < CACHE, slot[None, :] < cache_len[request], slot[None, :] - CACHE <= step_index[:, None])
        attention = attend(query_rows, all_keys, all_values, allowed)
        new_cache = jnp.stack([key_rows, value_rows], axis=2).reshape(DRAFT, -1)
        return (attention, new_cache)
    verify_attn, verify_cache = lax.map(one_request, jnp.arange(REQS, dtype=jnp.int32))

    def one_device(device):
        hidden_rows = lax.dynamic_slice_in_dim(prefill_x, device * PREF_DEV, PREF_DEV, 0)
        position, allowed = prompt_layout(prompt_len[device], PREF_DEV)
        query_rows, key_rows, value_rows = project(hidden_rows, attn_gain, w_query, w_keyval, qk_gain, position)
        attention = attend(query_rows, key_rows, value_rows, allowed)
        new_cache = jnp.stack([key_rows, value_rows], axis=2).reshape(PREF_DEV, -1)
        return (attention, new_cache)
    prefill_attn, prefill_cache = lax.map(one_device, jnp.arange(N_REQ, dtype=jnp.int32))
    all_rows = jnp.concatenate([verify_x.reshape(-1, D), prefill_x], axis=0)
    all_attn = jnp.concatenate([verify_attn.reshape(-1, HEADS * HEAD), prefill_attn.reshape(-1, HEADS * HEAD)], axis=0)
    projected = jnp.dot(all_attn, w_out, preferred_element_type=jnp.float32)
    final = (all_rows.astype(jnp.float32) + rms_scale(projected) * post_gain).astype(jnp.bfloat16)
    verify_out = final[:REQS * DRAFT].reshape(REQS, DRAFT, D)
    prefill_out = final[REQS * DRAFT:]
    keep_rows = jnp.arange(DRAFT, dtype=jnp.int32)[None, :, None] < accepted[:, None, None]
    verify_kv = jnp.where(keep_rows, verify_cache, jnp.zeros_like(verify_cache))
    prefill_kv = prefill_cache.reshape(PREFILL, -1)
    return (verify_out, prefill_out, verify_kv, prefill_kv)
```

```python
import functools

import jax
import jax.numpy as jnp
import numpy as np
from jax import lax
from jax.experimental import pallas as pl
from jax.experimental.pallas import tpu as pltpu
from jax.sharding import PartitionSpec as P

HEAD = 256
HALF = HEAD // 2
PAD = 16
SPAN = 256
eps_norm = 1e-06
rope_base = 1000000.0
neg_large = -1e30
MESH = pl.DeviceIdType.MESH


def rope_tables(longest):
    freq = rope_base ** (-2.0 * np.arange(HALF) / HEAD)
    low = np.arange(SPAN)[:, None] * freq[None, :]
    low = np.concatenate([np.cos(low), np.sin(low)], axis=1).astype(np.float32)
    coarse = low.astype(jnp.bfloat16)
    fine = (low - coarse.astype(np.float32)).astype(jnp.bfloat16)
    count = -(-(longest // SPAN + 1) // 8) * 8
    high = np.arange(count)[:, None] * float(SPAN) * freq[None, :]
    high = np.concatenate([np.cos(high), np.sin(high)], axis=1).astype(np.float32)
    return np.concatenate([coarse, fine], axis=1), high


def rms(values):
    return values * lax.rsqrt(jnp.mean(values * values, axis=-1, keepdims=True) + eps_norm)


def dot(a, b):
    return jnp.dot(a, b, preferred_element_type=jnp.float32)


def dot_t(a, b):
    return lax.dot_general(a, b, (((1,), (1,)), ((), ())), preferred_element_type=jnp.float32)


def kernel(
    n,
    outbound, page_table, cache_len, prompt_len, accepted,
    verify_x, prefill_x, attn_gain, w_query, w_keyval, qk_gain, w_out, post_gain,
    page_pool, table, high,
    verify_out, prefill_out, verify_kv, prefill_kv,
    x_v, vx_v, again_v, pgain_v, qkgain_v, table_v, high_v,
    wp_v, wo_v, pool_v, leaving, arrived, cached,
    normed, cos_v, sin_v, bias, kv_v, qv_v, attn_v, vattn_v,
    own_v, send_v, got_v, stat_v, gstat_v, vsend_v, vgot_v, out_v,
    local_sem, page_send, page_recv, ex_send, ex_recv,
):
    me = lax.axis_index("req")
    side = lax.axis_index("head")
    rows, width = x_v.shape
    draft = verify_x.shape[1]
    half = width // 2
    heads = attn_v.shape[1] // HEAD
    pages = page_table.shape[1]
    pool_pages = pool_v.shape[0]
    page_rows = pool_v.shape[1]
    mine = pl.multiple_of(side * half, half)
    theirs = pl.multiple_of((1 - side) * half, half)

    barrier = pltpu.get_barrier_semaphore()
    pl.semaphore_signal(barrier, inc=1, device_id=(me, 1 - side), device_id_type=MESH)

    def greet(step, carry):
        pl.semaphore_signal(
            barrier, inc=1, device_id=(lax.rem(me + step, n), side), device_id_type=MESH
        )
        return carry

    lax.fori_loop(1, n, greet, 0)

    copies = []

    def fetch(src, dst):
        copy = pltpu.make_async_copy(src, dst, local_sem.at[len(copies)])
        copy.start()
        copies.append(copy)
        return copy

    got_pool = fetch(page_pool, pool_v)
    got_x = fetch(prefill_x, x_v)
    got_again = fetch(attn_gain, again_v)
    got_w = [fetch(w_keyval.at[:, pl.ds(i * HEAD, HEAD)], wp_v.at[i]) for i in range(2)]
    got_table = fetch(table, table_v)
    got_high = fetch(high, high_v)
    got_qkgain = fetch(qk_gain, qkgain_v)
    got_w += [
        fetch(w_query.at[:, pl.ds(i * HEAD, HEAD)], wp_v.at[2 + i]) for i in range(heads)
    ]
    got_wo = [
        fetch(w_out.at[:, pl.ds(theirs, half)], wo_v.at[0]),
        fetch(w_out.at[:, pl.ds(mine, half)], wo_v.at[1]),
    ]
    got_pgain = fetch(post_gain, pgain_v)

    arrived[me] = jnp.zeros(arrived.shape[1:], arrived.dtype)
    got_pool.wait()

    def pack(d, carry):
        page = outbound[0, d]
        body = pool_v[jnp.clip(page, 0, pool_pages - 1)]
        leaving[d] = lax.select(page >= 0, body, jnp.zeros_like(body))
        return carry

    lax.fori_loop(0, n, pack, 0)

    vx_v[...] = jnp.zeros_like(vx_v)
    vx_v[0:draft, :] = verify_x[0].astype(jnp.float32)
    got_again.wait()
    normed[rows:, :] = (rms(vx_v[...]) * again_v[...]).astype(jnp.bfloat16)

    pl.semaphore_wait(barrier, n)

    def send(step, carry):
        d = lax.rem(me + step, n)
        pltpu.make_async_remote_copy(
            src_ref=leaving.at[d],
            dst_ref=arrived.at[me],
            send_sem=page_send.at[d],
            recv_sem=page_recv.at[me],
            device_id=(d, side),
            device_id_type=MESH,
        ).start()
        return carry

    lax.fori_loop(1, n, send, 0)

    got_x.wait()
    block = 32

    def norm_rows(i, carry):
        at = pl.ds(pl.multiple_of(i * block, block), block)
        normed[at, :] = (rms(x_v[at, :].astype(jnp.float32)) * again_v[...]).astype(jnp.bfloat16)
        return carry

    lax.fori_loop(0, rows // block, norm_rows, 0)

    row = lax.broadcasted_iota(jnp.int32, (rows, 1), 0)
    start = jnp.zeros((rows, 1), jnp.int32)
    end = jnp.int32(0)
    for k in range(prompt_len.shape[1] - 1):
        end = end + prompt_len[0, k]
        start = jnp.where(row >= end, end, start)
    col = lax.broadcasted_iota(jnp.int32, (rows, rows), 1)
    bias[...] = jnp.where((col <= row) & (col >= start), 0.0, neg_large)
    length = cache_len[0]
    vrow = lax.broadcasted_iota(jnp.int32, (PAD, 1), 0)
    vpos = length + jnp.minimum(vrow, draft - 1)
    lane = lax.broadcasted_iota(jnp.int32, (rows, SPAN), 1)
    vlane = lax.broadcasted_iota(jnp.int32, (PAD, SPAN), 1)
    got_table.wait()
    got_high.wait()
    got_qkgain.wait()

    def factors(pick):
        both = dot(jnp.where(pick, 1.0, 0.0).astype(jnp.bfloat16), table_v[...])
        return (
            both[:, :HALF] + both[:, HEAD:HEAD + HALF],
            both[:, HALF:HEAD] + both[:, HEAD + HALF:],
        )

    cos_p, sin_p = factors(lane == row - start)
    cos_v[0:rows, :] = cos_p
    sin_v[0:rows, :] = sin_p
    cos_l, sin_l = factors(vlane == jnp.bitwise_and(vpos, SPAN - 1))
    far = lax.shift_right_logical(vpos, 8)
    cos_h = jnp.zeros((PAD, HALF), jnp.float32)
    sin_h = jnp.zeros((PAD, HALF), jnp.float32)
    for k in range(high_v.shape[0]):
        cos_h = jnp.where(far == k, high_v[k:k + 1, :HALF], cos_h)
        sin_h = jnp.where(far == k, high_v[k:k + 1, HALF:], sin_h)
    cos_v[rows:, :] = cos_l * cos_h - sin_l * sin_h
    sin_v[rows:, :] = sin_l * cos_h + cos_l * sin_h

    def rope(values):
        first, second = values[:, :HALF], values[:, HALF:]
        cosine, sine = cos_v[...], sin_v[...]
        return jnp.concatenate(
            [first * cosine - second * sine, second * cosine + first * sine], axis=-1
        ).astype(jnp.bfloat16)

    got_w[0].wait()
    kv_v[:, :HEAD] = rope(rms(dot(normed[...], wp_v[0])) * qkgain_v[1:2, :])
    got_w[1].wait()
    kv_v[:, HEAD:] = rms(dot(normed[...], wp_v[1])).astype(jnp.bfloat16)
    put_kv = pltpu.make_async_copy(
        kv_v.at[pl.ds(0, rows)], prefill_kv, local_sem.at[len(copies)]
    )
    put_kv.start()
    vkv = kv_v[rows:, :].astype(jnp.float32)
    vkv = jnp.where(vrow < accepted[0], vkv, 0.0).astype(jnp.bfloat16)
    verify_kv[0] = vkv[0:draft, :]

    for i in range(heads):
        got_w[2 + i].wait()
        query = rope(rms(dot(normed[...], wp_v[2 + i])) * qkgain_v[0:1, :])
        qv_v[i * PAD:(i + 1) * PAD, :] = query[rows:, :]
        scores = dot_t(query[:rows, :], kv_v[:rows, :HEAD]) + bias[...]
        weights = jnp.exp(scores - jnp.max(scores, axis=-1, keepdims=True))
        probs = (weights / jnp.sum(weights, axis=-1, keepdims=True)).astype(jnp.bfloat16)
        attn_v[:, i * HEAD:(i + 1) * HEAD] = dot(probs, kv_v[:rows, HEAD:]).astype(jnp.bfloat16)

    def swap(src, dst, k):
        copy = pltpu.make_async_remote_copy(
            src_ref=src,
            dst_ref=dst,
            send_sem=ex_send.at[k],
            recv_sem=ex_recv.at[k],
            device_id=(me, 1 - side),
            device_id_type=MESH,
        )
        copy.start()
        return copy

    got_wo[0].wait()
    send_v[...] = dot(attn_v[...], wo_v[0]).astype(send_v.dtype)
    swap_rows = swap(send_v, got_v, 0)
    got_wo[1].wait()
    own_v[...] = dot(attn_v[...], wo_v[1])

    def arrive(step, carry):
        s = lax.rem(me + n - step, n)
        pltpu.make_async_remote_copy(
            src_ref=leaving.at[s],
            dst_ref=arrived.at[s],
            send_sem=page_send.at[s],
            recv_sem=page_recv.at[s],
            device_id=(s, side),
            device_id_type=MESH,
        ).wait()
        return carry

    lax.fori_loop(1, n, arrive, 0)

    def gather(i, carry):
        page = page_table[0, i]
        local = pool_v[jnp.minimum(page, pool_pages - 1)]
        moved = arrived[jnp.clip(page - pool_pages, 0, n - 1)]
        at = pl.ds(pl.multiple_of(i * page_rows, page_rows), page_rows)
        cached[at, :] = lax.select(page < pool_pages, local, moved)
        return carry

    lax.fori_loop(0, pages, gather, 0)

    queries = qv_v[...]
    old = dot_t(queries, cached[:, :HEAD])
    slot = lax.broadcasted_iota(jnp.int32, old.shape, 1)
    old = jnp.where(slot < length, old, neg_large)
    new = dot_t(queries, kv_v[rows:, :HEAD])
    step = jnp.bitwise_and(lax.broadcasted_iota(jnp.int32, new.shape, 0), PAD - 1)
    new = jnp.where(lax.broadcasted_iota(jnp.int32, new.shape, 1) <= step, new, neg_large)
    peak = jnp.maximum(
        jnp.max(old, axis=-1, keepdims=True), jnp.max(new, axis=-1, keepdims=True)
    )
    old = jnp.exp(old - peak)
    new = jnp.exp(new - peak)
    total = jnp.sum(old, axis=-1, keepdims=True) + jnp.sum(new, axis=-1, keepdims=True)
    mixed = dot((old / total).astype(jnp.bfloat16), cached[:, HEAD:])
    mixed = mixed + dot((new / total).astype(jnp.bfloat16), kv_v[rows:, HEAD:])
    mixed = mixed.astype(jnp.bfloat16)
    for i in range(heads):
        vattn_v[:, i * HEAD:(i + 1) * HEAD] = mixed[i * PAD:(i + 1) * PAD, :]

    swap_rows.wait()
    summed = own_v[...] + got_v[...].astype(jnp.float32)
    own_v[...] = summed
    stat_v[...] = jnp.broadcast_to(jnp.sum(summed * summed, axis=-1, keepdims=True), stat_v.shape)
    swap_stat = swap(stat_v, gstat_v, 1)

    vsend_v[0] = dot(vattn_v[...], wo_v[0])
    vsend_v[1] = dot(vattn_v[...], wo_v[1])
    swap_verify = swap(vsend_v, vgot_v, 2)

    got_pgain.wait()
    gain = pgain_v[:, pl.ds(mine, half)]
    swap_stat.wait()
    square = stat_v[:, 0:1] + gstat_v[:, 0:1]
    scale = lax.rsqrt(square / width + eps_norm)
    out_v[...] = (
        x_v[:, pl.ds(mine, half)].astype(jnp.float32) + own_v[...] * scale * gain
    ).astype(out_v.dtype)
    put_out = pltpu.make_async_copy(out_v, prefill_out, local_sem.at[len(copies) + 1])
    put_out.start()

    swap_verify.wait()
    ours = vsend_v[1] + vgot_v[0]
    other = vsend_v[0] + vgot_v[1]
    square = jnp.sum(ours * ours, axis=-1, keepdims=True)
    square = square + jnp.sum(other * other, axis=-1, keepdims=True)
    final = vx_v[:, pl.ds(mine, half)] + ours * lax.rsqrt(square / width + eps_norm) * gain
    verify_out[0] = final[0:draft, :].astype(verify_out.dtype)
    put_kv.wait()
    put_out.wait()


def on_device(
    verify_x, prefill_x, attn_gain, w_query, w_keyval, qk_gain, w_out, post_gain,
    page_pool, outbound, page_table, cache_len, prompt_len, accepted,
):
    n = lax.axis_size("req")
    _, draft, width = verify_x.shape
    rows = prefill_x.shape[0]
    all_rows = rows + PAD
    columns = w_query.shape[1]
    heads = columns // HEAD
    half = width // 2
    pages = page_table.shape[1]
    page = page_pool.shape[1:]
    table, high = rope_tables(pages * page[0] + draft)
    bf16, f32 = jnp.bfloat16, jnp.float32
    smem = pl.BlockSpec(memory_space=pltpu.SMEM)
    vmem = pl.BlockSpec(memory_space=pltpu.VMEM)
    hbm = pl.BlockSpec(memory_space=pl.ANY)
    fetched = 14 + heads
    return pl.pallas_call(
        functools.partial(kernel, n),
        out_shape=(
            jax.ShapeDtypeStruct((1, draft, half), bf16),
            jax.ShapeDtypeStruct((rows, half), bf16),
            jax.ShapeDtypeStruct((1, draft, 2 * HEAD), bf16),
            jax.ShapeDtypeStruct((rows, 2 * HEAD), bf16),
        ),
        in_specs=[smem] * 5 + [vmem] + [hbm] * 10,
        out_specs=(vmem, hbm, vmem, hbm),
        scratch_shapes=[
            pltpu.VMEM((rows, width), bf16),
            pltpu.VMEM((PAD, width), f32),
            pltpu.VMEM((1, width), f32),
            pltpu.VMEM((1, width), f32),
            pltpu.VMEM(qk_gain.shape, f32),
            pltpu.VMEM(table.shape, bf16),
            pltpu.VMEM(high.shape, f32),
            pltpu.VMEM((2 + heads, width, HEAD), bf16),
            pltpu.VMEM((2, columns, half), bf16),
            pltpu.VMEM(page_pool.shape, bf16),
            pltpu.VMEM((n,) + page, bf16),
            pltpu.VMEM((n,) + page, bf16),
            pltpu.VMEM((pages * page[0], page[1]), bf16),
            pltpu.VMEM((all_rows, width), bf16),
            pltpu.VMEM((all_rows, HALF), f32),
            pltpu.VMEM((all_rows, HALF), f32),
            pltpu.VMEM((rows, rows), f32),
            pltpu.VMEM((all_rows, 2 * HEAD), bf16),
            pltpu.VMEM((heads * PAD, HEAD), bf16),
            pltpu.VMEM((rows, columns), bf16),
            pltpu.VMEM((PAD, columns), bf16),
            pltpu.VMEM((rows, half), f32),
            pltpu.VMEM((rows, half), bf16),
            pltpu.VMEM((rows, half), bf16),
            pltpu.VMEM((rows, 128), f32),
            pltpu.VMEM((rows, 128), f32),
            pltpu.VMEM((2, PAD, half), f32),
            pltpu.VMEM((2, PAD, half), f32),
            pltpu.VMEM((rows, half), bf16),
            pltpu.SemaphoreType.DMA((fetched,)),
            pltpu.SemaphoreType.DMA((n,)),
            pltpu.SemaphoreType.DMA((n,)),
            pltpu.SemaphoreType.DMA((3,)),
            pltpu.SemaphoreType.DMA((3,)),
        ],
        compiler_params=pltpu.CompilerParams(
            collective_id=0, has_side_effects=True, vmem_limit_bytes=48 * 1024 * 1024
        ),
        cost_estimate=pl.CostEstimate(
            flops=2 * all_rows * width * (2 * columns + 2 * HEAD),
            bytes_accessed=16 * 1024 * 1024,
            transcendentals=heads * rows * rows,
        ),
    )(
        outbound, page_table, cache_len, prompt_len, accepted,
        verify_x, prefill_x, attn_gain.reshape(1, -1), w_query, w_keyval, qk_gain, w_out,
        post_gain.reshape(1, -1), page_pool, jnp.asarray(table), jnp.asarray(high),
    )


def solution(mesh):
    placed = (
        P("req", None, None),
        P("req", None),
        P(),
        P(None, "head"),
        P(None, "head"),
        P(),
        P("head", None),
        P(),
        P("req", None, "head"),
        P("req", None),
        P("req", None),
        P("req"),
        P("req", None),
        P("req"),
    )
    return jax.shard_map(
        on_device,
        mesh=mesh,
        in_specs=placed,
        out_specs=(
            P("req", None, "head"),
            P("req", "head"),
            P("req", None, "head"),
            P("req", "head"),
        ),
        check_vma=False,
    )
```

```python
import functools

import jax
import jax.numpy as jnp
import numpy as np
from jax import lax
from jax.experimental import pallas as pl
from jax.experimental.pallas import tpu as pltpu
from jax.sharding import PartitionSpec as P

HEAD = 256
HALF = HEAD // 2
VMEM_LIMIT = 62 * 1024 * 1024
PAD = 16
SPAN = 256
eps_norm = 1e-06
rope_base = 1000000.0
neg_large = -1e30
MESH = pl.DeviceIdType.MESH


def rope_tables(longest):
    freq = rope_base ** (-2.0 * np.arange(HALF) / HEAD)
    low = np.arange(SPAN)[:, None] * freq[None, :]
    low = np.concatenate([np.cos(low), np.sin(low)], axis=1).astype(np.float32)
    coarse = low.astype(jnp.bfloat16)
    fine = (low - coarse.astype(np.float32)).astype(jnp.bfloat16)
    count = -(-(longest // SPAN + 1) // 8) * 8
    high = np.arange(count)[:, None] * float(SPAN) * freq[None, :]
    high = np.concatenate([np.cos(high), np.sin(high)], axis=1).astype(np.float32)
    return np.concatenate([coarse, fine], axis=1), high


def rms(values):
    return values * lax.rsqrt(jnp.mean(values * values, axis=-1, keepdims=True) + eps_norm)


def dot(a, b):
    return jnp.dot(a, b, preferred_element_type=jnp.float32)


def dot_t(a, b):
    return lax.dot_general(a, b, (((1,), (1,)), ((), ())), preferred_element_type=jnp.float32)


def kernel(
    n,
    outbound_h, page_table_h, cache_len_h, prompt_len_h, accepted_h,
    verify_h, prefill_x, attn_gain, w_query, w_keyval, qk_gain, w_out, post_gain,
    page_pool, table, high,
    verify_out, prefill_out, verify_kv, prefill_kv,
    outbound, page_table, cache_len, prompt_len, accepted, verify_x,
    x_v, vx_v, again_v, pgain_v, qkgain_v, table_v, high_v,
    wp_v, wo_v, pool_v, leaving, arrived, cached,
    normed, cos_v, sin_v, bias, kv_v, qv_v, attn_v, vattn_v,
    own_v, send_v, got_v, stat_v, gstat_v, vsend_v, vgot_v, out_v, vout_v, vkv_v,
    local_sem, page_send, page_recv, ex_send, ex_recv,
):
    me = lax.axis_index("req")
    side = lax.axis_index("head")
    rows, width = x_v.shape
    draft = verify_x.shape[1]
    half = width // 2
    heads = attn_v.shape[1] // HEAD
    pages = page_table.shape[1]
    pool_pages = pool_v.shape[0]
    page_rows = pool_v.shape[1]
    mine = pl.multiple_of(side * half, half)
    theirs = pl.multiple_of((1 - side) * half, half)

    barrier = pltpu.get_barrier_semaphore()
    pl.semaphore_signal(barrier, inc=1, device_id=(me, 1 - side), device_id_type=MESH)

    def greet(step, carry):
        pl.semaphore_signal(
            barrier, inc=1, device_id=(lax.rem(me + step, n), side), device_id_type=MESH
        )
        return carry

    lax.fori_loop(1, n, greet, 0)

    copies = []

    def fetch(src, dst):
        copy = pltpu.make_async_copy(src, dst, local_sem.at[len(copies)])
        copy.start()
        copies.append(copy)
        return copy

    put = fetch
    got_outbound = fetch(outbound_h, outbound)
    got_pool = fetch(page_pool, pool_v)
    got_verify = fetch(verify_h, verify_x)
    got_again = fetch(attn_gain, again_v)
    got_x = fetch(prefill_x, x_v)
    got_small = [
        fetch(prompt_len_h, prompt_len),
        fetch(cache_len_h, cache_len),
        fetch(accepted_h, accepted),
        fetch(page_table_h, page_table),
    ]
    got_w = [fetch(w_keyval.at[:, pl.ds(i * HEAD, HEAD)], wp_v.at[i]) for i in range(2)]
    got_table = fetch(table, table_v)
    got_high = fetch(high, high_v)
    got_qkgain = fetch(qk_gain, qkgain_v)
    got_w += [
        fetch(w_query.at[:, pl.ds(i * HEAD, HEAD)], wp_v.at[2 + i]) for i in range(heads)
    ]
    got_wo = [
        fetch(w_out.at[:, pl.ds(theirs, half)], wo_v.at[0]),
        fetch(w_out.at[:, pl.ds(mine, half)], wo_v.at[1]),
    ]
    got_pgain = fetch(post_gain, pgain_v)

    arrived[me] = jnp.zeros(arrived.shape[1:], arrived.dtype)
    got_outbound.wait()
    got_pool.wait()

    def pack(d, carry):
        page = outbound[0, d]
        body = pool_v[jnp.clip(page, 0, pool_pages - 1)]
        leaving[d] = lax.select(page >= 0, body, jnp.zeros_like(body))
        return carry

    lax.fori_loop(0, n, pack, 0)

    vx_v[...] = jnp.zeros_like(vx_v)
    got_verify.wait()
    got_again.wait()
    vx_v[0:draft, :] = verify_x[0].astype(jnp.float32)
    normed[rows:, :] = (rms(vx_v[...]) * again_v[...]).astype(jnp.bfloat16)

    pl.semaphore_wait(barrier, n)

    def send(step, carry):
        d = lax.rem(me + step, n)
        pltpu.make_async_remote_copy(
            src_ref=leaving.at[d],
            dst_ref=arrived.at[me],
            send_sem=page_send.at[d],
            recv_sem=page_recv.at[me],
            device_id=(d, side),
            device_id_type=MESH,
        ).start()
        return carry

    lax.fori_loop(1, n, send, 0)

    got_x.wait()
    block = 32

    def norm_rows(i, carry):
        at = pl.ds(pl.multiple_of(i * block, block), block)
        normed[at, :] = (rms(x_v[at, :].astype(jnp.float32)) * again_v[...]).astype(jnp.bfloat16)
        return carry

    lax.fori_loop(0, rows // block, norm_rows, 0)

    for copy in got_small:
        copy.wait()
    row = lax.broadcasted_iota(jnp.int32, (rows, 1), 0)
    start = jnp.zeros((rows, 1), jnp.int32)
    end = jnp.int32(0)
    for k in range(prompt_len.shape[1] - 1):
        end = end + prompt_len[0, k]
        start = jnp.where(row >= end, end, start)
    col = lax.broadcasted_iota(jnp.int32, (rows, rows), 1)
    bias[...] = jnp.where((col <= row) & (col >= start), 0.0, neg_large)
    length = cache_len[0, 0]
    vrow = lax.broadcasted_iota(jnp.int32, (PAD, 1), 0)
    vpos = length + jnp.minimum(vrow, draft - 1)
    lane = lax.broadcasted_iota(jnp.int32, (rows, SPAN), 1)
    vlane = lax.broadcasted_iota(jnp.int32, (PAD, SPAN), 1)
    got_table.wait()
    got_high.wait()
    got_qkgain.wait()

    def factors(pick):
        both = dot(jnp.where(pick, 1.0, 0.0).astype(jnp.bfloat16), table_v[...])
        return (
            both[:, :HALF] + both[:, HEAD:HEAD + HALF],
            both[:, HALF:HEAD] + both[:, HEAD + HALF:],
        )

    cos_p, sin_p = factors(lane == row - start)
    cos_v[0:rows, :] = cos_p
    sin_v[0:rows, :] = sin_p
    cos_l, sin_l = factors(vlane == jnp.bitwise_and(vpos, SPAN - 1))
    far = lax.shift_right_logical(vpos, 8)
    cos_h = jnp.zeros((PAD, HALF), jnp.float32)
    sin_h = jnp.zeros((PAD, HALF), jnp.float32)
    for k in range(high_v.shape[0]):
        cos_h = jnp.where(far == k, high_v[k:k + 1, :HALF], cos_h)
        sin_h = jnp.where(far == k, high_v[k:k + 1, HALF:], sin_h)
    cos_v[rows:, :] = cos_l * cos_h - sin_l * sin_h
    sin_v[rows:, :] = sin_l * cos_h + cos_l * sin_h

    def rope(values):
        first, second = values[:, :HALF], values[:, HALF:]
        cosine, sine = cos_v[...], sin_v[...]
        return jnp.concatenate(
            [first * cosine - second * sine, second * cosine + first * sine], axis=-1
        ).astype(jnp.bfloat16)

    got_w[0].wait()
    kv_v[:, :HEAD] = rope(rms(dot(normed[...], wp_v[0])) * qkgain_v[1:2, :])
    got_w[1].wait()
    kv_v[:, HEAD:] = rms(dot(normed[...], wp_v[1])).astype(jnp.bfloat16)
    put_kv = put(kv_v.at[pl.ds(0, rows)], prefill_kv)
    vkv = kv_v[rows:, :].astype(jnp.float32)
    vkv = jnp.where(vrow < accepted[0, 0], vkv, 0.0).astype(jnp.bfloat16)
    vkv_v[0] = vkv[0:draft, :]
    put_vkv = put(vkv_v, verify_kv)

    for i in range(heads):
        got_w[2 + i].wait()
        query = rope(rms(dot(normed[...], wp_v[2 + i])) * qkgain_v[0:1, :])
        qv_v[i * PAD:(i + 1) * PAD, :] = query[rows:, :]
        scores = dot_t(query[:rows, :], kv_v[:rows, :HEAD]) + bias[...]
        weights = jnp.exp(scores - jnp.max(scores, axis=-1, keepdims=True))
        share = 1.0 / jnp.sum(weights, axis=-1, keepdims=True)
        probs = (weights * share).astype(jnp.bfloat16)
        attn_v[:, i * HEAD:(i + 1) * HEAD] = dot(probs, kv_v[:rows, HEAD:]).astype(jnp.bfloat16)

    def swap(src, dst, k):
        copy = pltpu.make_async_remote_copy(
            src_ref=src,
            dst_ref=dst,
            send_sem=ex_send.at[k],
            recv_sem=ex_recv.at[k],
            device_id=(me, 1 - side),
            device_id_type=MESH,
        )
        copy.start()
        return copy

    got_wo[0].wait()
    send_v[...] = dot(attn_v[...], wo_v[0]).astype(send_v.dtype)
    swap_rows = swap(send_v, got_v, 0)
    got_wo[1].wait()
    own_v[...] = dot(attn_v[...], wo_v[1])

    def arrive(step, carry):
        s = lax.rem(me + n - step, n)
        pltpu.make_async_remote_copy(
            src_ref=leaving.at[s],
            dst_ref=arrived.at[s],
            send_sem=page_send.at[s],
            recv_sem=page_recv.at[s],
            device_id=(s, side),
            device_id_type=MESH,
        ).wait()
        return carry

    lax.fori_loop(1, n, arrive, 0)

    def gather(i, carry):
        page = page_table[0, i]
        local = pool_v[jnp.minimum(page, pool_pages - 1)]
        moved = arrived[jnp.clip(page - pool_pages, 0, n - 1)]
        at = pl.ds(pl.multiple_of(i * page_rows, page_rows), page_rows)
        cached[at, :] = lax.select(page < pool_pages, local, moved)
        return carry

    lax.fori_loop(0, pages, gather, 0)

    queries = qv_v[...]
    old = dot_t(queries, cached[:, :HEAD])
    slot = lax.broadcasted_iota(jnp.int32, old.shape, 1)
    old = jnp.where(slot < length, old, neg_large)
    new = dot_t(queries, kv_v[rows:, :HEAD])
    step = jnp.bitwise_and(lax.broadcasted_iota(jnp.int32, new.shape, 0), PAD - 1)
    new = jnp.where(lax.broadcasted_iota(jnp.int32, new.shape, 1) <= step, new, neg_large)
    peak = jnp.maximum(
        jnp.max(old, axis=-1, keepdims=True), jnp.max(new, axis=-1, keepdims=True)
    )
    old = jnp.exp(old - peak)
    new = jnp.exp(new - peak)
    share = 1.0 / (jnp.sum(old, axis=-1, keepdims=True) + jnp.sum(new, axis=-1, keepdims=True))
    mixed = dot((old * share).astype(jnp.bfloat16), cached[:, HEAD:])
    mixed = mixed + dot((new * share).astype(jnp.bfloat16), kv_v[rows:, HEAD:])
    mixed = mixed.astype(jnp.bfloat16)
    for i in range(heads):
        vattn_v[:, i * HEAD:(i + 1) * HEAD] = mixed[i * PAD:(i + 1) * PAD, :]

    swap_rows.wait()
    summed = own_v[...] + got_v[...].astype(jnp.float32)
    own_v[...] = summed
    stat_v[...] = jnp.broadcast_to(jnp.sum(summed * summed, axis=-1, keepdims=True), stat_v.shape)
    swap_stat = swap(stat_v, gstat_v, 1)

    vsend_v[0] = dot(vattn_v[...], wo_v[0])
    vsend_v[1] = dot(vattn_v[...], wo_v[1])
    swap_verify = swap(vsend_v, vgot_v, 2)

    got_pgain.wait()
    gain = pgain_v[:, pl.ds(mine, half)]
    swap_stat.wait()
    square = stat_v[:, 0:1] + gstat_v[:, 0:1]
    scale = lax.rsqrt(square / width + eps_norm)
    out_v[...] = (
        x_v[:, pl.ds(mine, half)].astype(jnp.float32) + own_v[...] * scale * gain
    ).astype(out_v.dtype)
    put_out = put(out_v, prefill_out)

    swap_verify.wait()
    ours = vsend_v[1] + vgot_v[0]
    other = vsend_v[0] + vgot_v[1]
    square = jnp.sum(ours * ours, axis=-1, keepdims=True)
    square = square + jnp.sum(other * other, axis=-1, keepdims=True)
    final = vx_v[:, pl.ds(mine, half)] + ours * lax.rsqrt(square / width + eps_norm) * gain
    vout_v[0] = final[0:draft, :].astype(vout_v.dtype)
    put_vout = put(vout_v, verify_out)
    for copy in (put_kv, put_vkv, put_out, put_vout):
        copy.wait()


def write_out(*refs):
    count = len(refs) // 2
    sems = refs[-1]
    copies = [
        pltpu.make_async_copy(refs[k], refs[count + k], sems.at[k]) for k in range(count)
    ]
    for copy in copies:
        copy.start()
    for copy in copies:
        copy.wait()


def on_device(
    verify_x, prefill_x, attn_gain, w_query, w_keyval, qk_gain, w_out, post_gain,
    page_pool, outbound, page_table, cache_len, prompt_len, accepted,
):
    n = lax.axis_size("req")
    _, draft, width = verify_x.shape
    rows = prefill_x.shape[0]
    all_rows = rows + PAD
    columns = w_query.shape[1]
    heads = columns // HEAD
    half = width // 2
    pages = page_table.shape[1]
    page = page_pool.shape[1:]
    table, high = rope_tables(pages * page[0] + draft)
    bf16, f32 = jnp.bfloat16, jnp.float32
    hbm = pl.BlockSpec(memory_space=pltpu.HBM)
    moved = 21 + heads
    results = pl.pallas_call(
        functools.partial(kernel, n),
        out_shape=(
            jax.ShapeDtypeStruct((1, draft, half), bf16),
            jax.ShapeDtypeStruct((rows, half), bf16),
            jax.ShapeDtypeStruct((1, draft, 2 * HEAD), bf16),
            jax.ShapeDtypeStruct((rows, 2 * HEAD), bf16),
        ),
        in_specs=[hbm] * 16,
        out_specs=(hbm,) * 4,
        scratch_shapes=[
            pltpu.SMEM(outbound.shape, jnp.int32),
            pltpu.SMEM(page_table.shape, jnp.int32),
            pltpu.SMEM((1, 1), jnp.int32),
            pltpu.SMEM(prompt_len.shape, jnp.int32),
            pltpu.SMEM((1, 1), jnp.int32),
            pltpu.VMEM(verify_x.shape, bf16),
            pltpu.VMEM((rows, width), bf16),
            pltpu.VMEM((PAD, width), f32),
            pltpu.VMEM((1, width), f32),
            pltpu.VMEM((1, width), f32),
            pltpu.VMEM(qk_gain.shape, f32),
            pltpu.VMEM(table.shape, bf16),
            pltpu.VMEM(high.shape, f32),
            pltpu.VMEM((2 + heads, width, HEAD), bf16),
            pltpu.VMEM((2, columns, half), bf16),
            pltpu.VMEM(page_pool.shape, bf16),
            pltpu.VMEM((n,) + page, bf16),
            pltpu.VMEM((n,) + page, bf16),
            pltpu.VMEM((pages * page[0], page[1]), bf16),
            pltpu.VMEM((all_rows, width), bf16),
            pltpu.VMEM((all_rows, HALF), f32),
            pltpu.VMEM((all_rows, HALF), f32),
            pltpu.VMEM((rows, rows), f32),
            pltpu.VMEM((all_rows, 2 * HEAD), bf16),
            pltpu.VMEM((heads * PAD, HEAD), bf16),
            pltpu.VMEM((rows, columns), bf16),
            pltpu.VMEM((PAD, columns), bf16),
            pltpu.VMEM((rows, half), f32),
            pltpu.VMEM((rows, half), bf16),
            pltpu.VMEM((rows, half), bf16),
            pltpu.VMEM((rows, 128), f32),
            pltpu.VMEM((rows, 128), f32),
            pltpu.VMEM((2, PAD, half), f32),
            pltpu.VMEM((2, PAD, half), f32),
            pltpu.VMEM((rows, half), bf16),
            pltpu.VMEM((1, draft, half), bf16),
            pltpu.VMEM((1, draft, 2 * HEAD), bf16),
            pltpu.SemaphoreType.DMA((moved,)),
            pltpu.SemaphoreType.DMA((n,)),
            pltpu.SemaphoreType.DMA((n,)),
            pltpu.SemaphoreType.DMA((3,)),
            pltpu.SemaphoreType.DMA((3,)),
        ],
        compiler_params=pltpu.CompilerParams(
            collective_id=0, has_side_effects=True, vmem_limit_bytes=VMEM_LIMIT
        ),
        cost_estimate=pl.CostEstimate(
            flops=2 * all_rows * width * (2 * columns + 2 * HEAD),
            bytes_accessed=16 * 1024 * 1024,
            transcendentals=heads * rows * rows,
        ),
    )(
        outbound, page_table, cache_len[None], prompt_len, accepted[None],
        verify_x, prefill_x, attn_gain.reshape(1, -1), w_query, w_keyval, qk_gain, w_out,
        post_gain.reshape(1, -1), page_pool, jnp.asarray(table), jnp.asarray(high),
    )
    return pl.pallas_call(
        write_out,
        out_shape=tuple(jax.ShapeDtypeStruct(r.shape, r.dtype) for r in results),
        in_specs=[pl.BlockSpec(memory_space=pl.ANY)] * 4,
        out_specs=(hbm,) * 4,
        scratch_shapes=[pltpu.SemaphoreType.DMA((4,))],
        compiler_params=pltpu.CompilerParams(vmem_limit_bytes=VMEM_LIMIT),
    )(*results)


def solution(mesh):
    placed = (
        P("req", None, None),
        P("req", None),
        P(),
        P(None, "head"),
        P(None, "head"),
        P(),
        P("head", None),
        P(),
        P("req", None, "head"),
        P("req", None),
        P("req", None),
        P("req"),
        P("req", None),
        P("req"),
    )
    return jax.shard_map(
        on_device,
        mesh=mesh,
        in_specs=placed,
        out_specs=(
            P("req", None, "head"),
            P("req", "head"),
            P("req", None, "head"),
            P("req", "head"),
        ),
        check_vma=False,
    )
```

```python
import functools

import jax
import jax.numpy as jnp
import numpy as np
from jax import lax
from jax.experimental import pallas as pl
from jax.experimental.pallas import tpu as pltpu
from jax.sharding import PartitionSpec as P

HEAD = 256
HALF = HEAD // 2
VMEM_LIMIT = 62 * 1024 * 1024
PAD = 16
SPAN = 256
eps_norm = 1e-06
rope_base = 1000000.0
neg_large = -1e30
MESH = pl.DeviceIdType.MESH


def rope_tables(longest):
    freq = rope_base ** (-2.0 * np.arange(HALF) / HEAD)
    low = np.arange(SPAN)[:, None] * freq[None, :]
    low = np.concatenate([np.cos(low), np.sin(low)], axis=1).astype(np.float32)
    coarse = low.astype(jnp.bfloat16)
    fine = (low - coarse.astype(np.float32)).astype(jnp.bfloat16)
    count = -(-(longest // SPAN + 1) // 8) * 8
    high = np.arange(count)[:, None] * float(SPAN) * freq[None, :]
    high = np.concatenate([np.cos(high), np.sin(high)], axis=1).astype(np.float32)
    return np.concatenate([coarse, fine], axis=1), high


def rms(values):
    return values * lax.rsqrt(jnp.mean(values * values, axis=-1, keepdims=True) + eps_norm)


def dot(a, b):
    return jnp.dot(a, b, preferred_element_type=jnp.float32)


def dot_t(a, b):
    return lax.dot_general(a, b, (((1,), (1,)), ((), ())), preferred_element_type=jnp.float32)


def kernel(
    n,
    outbound_h, page_table_h, cache_len_h, prompt_len_h, accepted_h,
    verify_h, prefill_x, attn_gain, w_query, w_keyval, qk_gain, w_out, post_gain,
    page_pool, table, high,
    verify_out, prefill_out, verify_kv, prefill_kv,
    outbound, page_table, cache_len, prompt_len, accepted, verify_x,
    x_v, vx_v, again_v, pgain_v, qkgain_v, table_v, high_v,
    wp_v, wo_v, pool_v, leaving, arrived, cached,
    normed, cos_v, sin_v, bias, kv_v, qv_v, attn_v, vattn_v,
    own_v, send_v, got_v, stat_v, gstat_v, vsend_v, vgot_v, out_v, vout_v, vkv_v,
    local_sem, page_send, page_recv, ex_send, ex_recv,
):
    me = lax.axis_index("req")
    side = lax.axis_index("head")
    rows, width = x_v.shape
    draft = verify_x.shape[1]
    half = width // 2
    heads = attn_v.shape[1] // HEAD
    pages = page_table.shape[1]
    pool_pages = pool_v.shape[0]
    page_rows = pool_v.shape[1]
    mine = pl.multiple_of(side * half, half)
    theirs = pl.multiple_of((1 - side) * half, half)

    barrier = pltpu.get_barrier_semaphore()
    pl.semaphore_signal(barrier, inc=1, device_id=(me, 1 - side), device_id_type=MESH)

    def greet(step, carry):
        pl.semaphore_signal(
            barrier, inc=1, device_id=(lax.rem(me + step, n), side), device_id_type=MESH
        )
        return carry

    lax.fori_loop(1, n, greet, 0)

    copies = []

    def fetch(src, dst):
        copy = pltpu.make_async_copy(src, dst, local_sem.at[len(copies)])
        copy.start()
        copies.append(copy)
        return copy

    put = fetch
    got_again = fetch(attn_gain, again_v)
    got_verify = fetch(verify_h, verify_x)
    got_x = fetch(prefill_x, x_v)
    got_outbound = fetch(outbound_h, outbound)
    got_small = [
        fetch(prompt_len_h, prompt_len),
        fetch(cache_len_h, cache_len),
        fetch(accepted_h, accepted),
        fetch(page_table_h, page_table),
    ]
    got_w = [fetch(w_keyval.at[:, pl.ds(i * HEAD, HEAD)], wp_v.at[i]) for i in range(2)]
    got_pool = fetch(page_pool, pool_v)
    got_table = fetch(table, table_v)
    got_high = fetch(high, high_v)
    got_qkgain = fetch(qk_gain, qkgain_v)
    got_w += [
        fetch(w_query.at[:, pl.ds(i * HEAD, HEAD)], wp_v.at[2 + i]) for i in range(heads)
    ]
    got_wo = [
        fetch(w_out.at[:, pl.ds(theirs, half)], wo_v.at[0]),
        fetch(w_out.at[:, pl.ds(mine, half)], wo_v.at[1]),
    ]
    got_pgain = fetch(post_gain, pgain_v)

    vx_v[...] = jnp.zeros_like(vx_v)
    got_verify.wait()
    got_again.wait()
    vx_v[0:draft, :] = verify_x[0].astype(jnp.float32)
    normed[rows:, :] = (rms(vx_v[...]) * again_v[...]).astype(jnp.bfloat16)

    got_x.wait()
    block = 32

    def norm_rows(i, carry):
        at = pl.ds(pl.multiple_of(i * block, block), block)
        normed[at, :] = (rms(x_v[at, :].astype(jnp.float32)) * again_v[...]).astype(jnp.bfloat16)
        return carry

    lax.fori_loop(0, rows // block, norm_rows, 0)

    for copy in got_small:
        copy.wait()
    row = lax.broadcasted_iota(jnp.int32, (rows, 1), 0)
    start = jnp.zeros((rows, 1), jnp.int32)
    end = jnp.int32(0)
    for k in range(prompt_len.shape[1] - 1):
        end = end + prompt_len[0, k]
        start = jnp.where(row >= end, end, start)
    col = lax.broadcasted_iota(jnp.int32, (rows, rows), 1)
    bias[...] = jnp.where((col <= row) & (col >= start), 0.0, neg_large)
    length = cache_len[0, 0]
    vrow = lax.broadcasted_iota(jnp.int32, (PAD, 1), 0)
    vpos = length + jnp.minimum(vrow, draft - 1)
    lane = lax.broadcasted_iota(jnp.int32, (rows, SPAN), 1)
    vlane = lax.broadcasted_iota(jnp.int32, (PAD, SPAN), 1)
    got_table.wait()
    got_high.wait()
    got_qkgain.wait()

    def factors(pick):
        both = dot(jnp.where(pick, 1.0, 0.0).astype(jnp.bfloat16), table_v[...])
        return (
            both[:, :HALF] + both[:, HEAD:HEAD + HALF],
            both[:, HALF:HEAD] + both[:, HEAD + HALF:],
        )

    cos_p, sin_p = factors(lane == row - start)
    cos_v[0:rows, :] = cos_p
    sin_v[0:rows, :] = sin_p
    cos_l, sin_l = factors(vlane == jnp.bitwise_and(vpos, SPAN - 1))
    far = lax.shift_right_logical(vpos, 8)
    cos_h = jnp.zeros((PAD, HALF), jnp.float32)
    sin_h = jnp.zeros((PAD, HALF), jnp.float32)
    for k in range(high_v.shape[0]):
        cos_h = jnp.where(far == k, high_v[k:k + 1, :HALF], cos_h)
        sin_h = jnp.where(far == k, high_v[k:k + 1, HALF:], sin_h)
    cos_v[rows:, :] = cos_l * cos_h - sin_l * sin_h
    sin_v[rows:, :] = sin_l * cos_h + cos_l * sin_h

    def rope(values):
        first, second = values[:, :HALF], values[:, HALF:]
        cosine, sine = cos_v[...], sin_v[...]
        return jnp.concatenate(
            [first * cosine - second * sine, second * cosine + first * sine], axis=-1
        ).astype(jnp.bfloat16)

    got_w[0].wait()
    kv_v[:, :HEAD] = rope(rms(dot(normed[...], wp_v[0])) * qkgain_v[1:2, :])
    got_w[1].wait()
    kv_v[:, HEAD:] = rms(dot(normed[...], wp_v[1])).astype(jnp.bfloat16)
    put_kv = put(kv_v.at[pl.ds(0, rows)], prefill_kv)
    vkv = kv_v[rows:, :].astype(jnp.float32)
    vkv = jnp.where(vrow < accepted[0, 0], vkv, 0.0).astype(jnp.bfloat16)
    vkv_v[0] = vkv[0:draft, :]
    put_vkv = put(vkv_v, verify_kv)

    arrived[me] = jnp.zeros(arrived.shape[1:], arrived.dtype)
    got_outbound.wait()
    got_pool.wait()

    def pack(d, carry):
        page = outbound[0, d]
        body = pool_v[jnp.clip(page, 0, pool_pages - 1)]
        leaving[d] = lax.select(page >= 0, body, jnp.zeros_like(body))
        return carry

    lax.fori_loop(0, n, pack, 0)

    for copy in got_w[2:]:
        copy.wait()

    def project(i):
        query = rope(rms(dot(normed[...], wp_v[2 + i])) * qkgain_v[0:1, :])
        qv_v[i * PAD:(i + 1) * PAD, :] = query[rows:, :]
        return query

    ahead = project(0)

    pl.semaphore_wait(barrier, n)

    def send(step, carry):
        d = lax.rem(me + step, n)
        pltpu.make_async_remote_copy(
            src_ref=leaving.at[d],
            dst_ref=arrived.at[me],
            send_sem=page_send.at[d],
            recv_sem=page_recv.at[me],
            device_id=(d, side),
            device_id_type=MESH,
        ).start()
        return carry

    lax.fori_loop(1, n, send, 0)

    for i in range(heads):
        query = ahead
        if i + 1 < heads:
            ahead = project(i + 1)
        scores = dot_t(query[:rows, :], kv_v[:rows, :HEAD]) + bias[...]
        weights = jnp.exp(scores - jnp.max(scores, axis=-1, keepdims=True))
        share = 1.0 / jnp.sum(weights, axis=-1, keepdims=True)
        probs = (weights * share).astype(jnp.bfloat16)
        attn_v[:, i * HEAD:(i + 1) * HEAD] = dot(probs, kv_v[:rows, HEAD:]).astype(jnp.bfloat16)

    def swap(src, dst, k):
        copy = pltpu.make_async_remote_copy(
            src_ref=src,
            dst_ref=dst,
            send_sem=ex_send.at[k],
            recv_sem=ex_recv.at[k],
            device_id=(me, 1 - side),
            device_id_type=MESH,
        )
        copy.start()
        return copy

    got_wo[0].wait()
    send_v[...] = dot(attn_v[...], wo_v[0]).astype(send_v.dtype)
    swap_rows = swap(send_v, got_v, 0)
    got_wo[1].wait()
    own_v[...] = dot(attn_v[...], wo_v[1])

    def arrive(step, carry):
        s = lax.rem(me + n - step, n)
        pltpu.make_async_remote_copy(
            src_ref=leaving.at[s],
            dst_ref=arrived.at[s],
            send_sem=page_send.at[s],
            recv_sem=page_recv.at[s],
            device_id=(s, side),
            device_id_type=MESH,
        ).wait()
        return carry

    lax.fori_loop(1, n, arrive, 0)

    def gather(i, carry):
        page = page_table[0, i]
        local = pool_v[jnp.minimum(page, pool_pages - 1)]
        moved = arrived[jnp.clip(page - pool_pages, 0, n - 1)]
        at = pl.ds(pl.multiple_of(i * page_rows, page_rows), page_rows)
        cached[at, :] = lax.select(page < pool_pages, local, moved)
        return carry

    lax.fori_loop(0, pages, gather, 0)

    queries = qv_v[...]
    old = dot_t(queries, cached[:, :HEAD])
    slot = lax.broadcasted_iota(jnp.int32, old.shape, 1)
    old = jnp.where(slot < length, old, neg_large)
    new = dot_t(queries, kv_v[rows:, :HEAD])
    step = jnp.bitwise_and(lax.broadcasted_iota(jnp.int32, new.shape, 0), PAD - 1)
    new = jnp.where(lax.broadcasted_iota(jnp.int32, new.shape, 1) <= step, new, neg_large)
    peak = jnp.maximum(
        jnp.max(old, axis=-1, keepdims=True), jnp.max(new, axis=-1, keepdims=True)
    )
    old = jnp.exp(old - peak)
    new = jnp.exp(new - peak)
    share = 1.0 / (jnp.sum(old, axis=-1, keepdims=True) + jnp.sum(new, axis=-1, keepdims=True))
    mixed = dot((old * share).astype(jnp.bfloat16), cached[:, HEAD:])
    mixed = mixed + dot((new * share).astype(jnp.bfloat16), kv_v[rows:, HEAD:])
    mixed = mixed.astype(jnp.bfloat16)
    for i in range(heads):
        vattn_v[:, i * HEAD:(i + 1) * HEAD] = mixed[i * PAD:(i + 1) * PAD, :]

    swap_rows.wait()
    summed = own_v[...] + got_v[...].astype(jnp.float32)
    own_v[...] = summed
    stat_v[...] = jnp.broadcast_to(jnp.sum(summed * summed, axis=-1, keepdims=True), stat_v.shape)
    swap_stat = swap(stat_v, gstat_v, 1)

    vsend_v[0] = dot(vattn_v[...], wo_v[0])
    vsend_v[1] = dot(vattn_v[...], wo_v[1])
    swap_verify = swap(vsend_v, vgot_v, 2)

    got_pgain.wait()
    gain = pgain_v[:, pl.ds(mine, half)]
    swap_stat.wait()
    square = stat_v[:, 0:1] + gstat_v[:, 0:1]
    scale = lax.rsqrt(square / width + eps_norm)
    out_v[...] = (
        x_v[:, pl.ds(mine, half)].astype(jnp.float32) + own_v[...] * scale * gain
    ).astype(out_v.dtype)
    put_out = put(out_v, prefill_out)

    swap_verify.wait()
    ours = vsend_v[1] + vgot_v[0]
    other = vsend_v[0] + vgot_v[1]
    square = jnp.sum(ours * ours, axis=-1, keepdims=True)
    square = square + jnp.sum(other * other, axis=-1, keepdims=True)
    final = vx_v[:, pl.ds(mine, half)] + ours * lax.rsqrt(square / width + eps_norm) * gain
    vout_v[0] = final[0:draft, :].astype(vout_v.dtype)
    put_vout = put(vout_v, verify_out)
    for copy in (put_kv, put_vkv, put_out, put_vout):
        copy.wait()


def write_out(count, *refs):
    sources, results, held = refs[:count], refs[count:2 * count], refs[2 * count:3 * count]
    in_sem, out_sem = refs[3 * count:]
    ins = [pltpu.make_async_copy(sources[k], held[k], in_sem.at[k]) for k in range(count)]
    outs = [pltpu.make_async_copy(held[k], results[k], out_sem.at[k]) for k in range(count)]
    for copy in ins:
        copy.start()
    for k in range(count):
        ins[k].wait()
        outs[k].start()
    for copy in outs:
        copy.wait()


def on_device(
    verify_x, prefill_x, attn_gain, w_query, w_keyval, qk_gain, w_out, post_gain,
    page_pool, outbound, page_table, cache_len, prompt_len, accepted,
):
    n = lax.axis_size("req")
    _, draft, width = verify_x.shape
    rows = prefill_x.shape[0]
    all_rows = rows + PAD
    columns = w_query.shape[1]
    heads = columns // HEAD
    half = width // 2
    pages = page_table.shape[1]
    page = page_pool.shape[1:]
    table, high = rope_tables(pages * page[0] + draft)
    bf16, f32 = jnp.bfloat16, jnp.float32
    hbm = pl.BlockSpec(memory_space=pltpu.HBM)
    moved = 21 + heads
    results = pl.pallas_call(
        functools.partial(kernel, n),
        out_shape=(
            jax.ShapeDtypeStruct((1, draft, half), bf16),
            jax.ShapeDtypeStruct((rows, half), bf16),
            jax.ShapeDtypeStruct((1, draft, 2 * HEAD), bf16),
            jax.ShapeDtypeStruct((rows, 2 * HEAD), bf16),
        ),
        in_specs=[hbm] * 16,
        out_specs=(hbm,) * 4,
        scratch_shapes=[
            pltpu.SMEM(outbound.shape, jnp.int32),
            pltpu.SMEM(page_table.shape, jnp.int32),
            pltpu.SMEM((1, 1), jnp.int32),
            pltpu.SMEM(prompt_len.shape, jnp.int32),
            pltpu.SMEM((1, 1), jnp.int32),
            pltpu.VMEM(verify_x.shape, bf16),
            pltpu.VMEM((rows, width), bf16),
            pltpu.VMEM((PAD, width), f32),
            pltpu.VMEM((1, width), f32),
            pltpu.VMEM((1, width), f32),
            pltpu.VMEM(qk_gain.shape, f32),
            pltpu.VMEM(table.shape, bf16),
            pltpu.VMEM(high.shape, f32),
            pltpu.VMEM((2 + heads, width, HEAD), bf16),
            pltpu.VMEM((2, columns, half), bf16),
            pltpu.VMEM(page_pool.shape, bf16),
            pltpu.VMEM((n,) + page, bf16),
            pltpu.VMEM((n,) + page, bf16),
            pltpu.VMEM((pages * page[0], page[1]), bf16),
            pltpu.VMEM((all_rows, width), bf16),
            pltpu.VMEM((all_rows, HALF), f32),
            pltpu.VMEM((all_rows, HALF), f32),
            pltpu.VMEM((rows, rows), f32),
            pltpu.VMEM((all_rows, 2 * HEAD), bf16),
            pltpu.VMEM((heads * PAD, HEAD), bf16),
            pltpu.VMEM((rows, columns), bf16),
            pltpu.VMEM((PAD, columns), bf16),
            pltpu.VMEM((rows, half), f32),
            pltpu.VMEM((rows, half), bf16),
            pltpu.VMEM((rows, half), bf16),
            pltpu.VMEM((rows, 128), f32),
            pltpu.VMEM((rows, 128), f32),
            pltpu.VMEM((2, PAD, half), f32),
            pltpu.VMEM((2, PAD, half), f32),
            pltpu.VMEM((rows, half), bf16),
            pltpu.VMEM((1, draft, half), bf16),
            pltpu.VMEM((1, draft, 2 * HEAD), bf16),
            pltpu.SemaphoreType.DMA((moved,)),
            pltpu.SemaphoreType.DMA((n,)),
            pltpu.SemaphoreType.DMA((n,)),
            pltpu.SemaphoreType.DMA((3,)),
            pltpu.SemaphoreType.DMA((3,)),
        ],
        compiler_params=pltpu.CompilerParams(
            collective_id=0, has_side_effects=True, vmem_limit_bytes=VMEM_LIMIT
        ),
        cost_estimate=pl.CostEstimate(
            flops=2 * all_rows * width * (2 * columns + 2 * HEAD),
            bytes_accessed=16 * 1024 * 1024,
            transcendentals=heads * rows * rows,
        ),
    )(
        outbound, page_table, cache_len[None], prompt_len, accepted[None],
        verify_x, prefill_x, attn_gain.reshape(1, -1), w_query, w_keyval, qk_gain, w_out,
        post_gain.reshape(1, -1), page_pool, jnp.asarray(table), jnp.asarray(high),
    )
    return pl.pallas_call(
        functools.partial(write_out, len(results)),
        out_shape=tuple(jax.ShapeDtypeStruct(r.shape, r.dtype) for r in results),
        in_specs=[pl.BlockSpec(memory_space=pl.ANY)] * 4,
        out_specs=(hbm,) * 4,
        scratch_shapes=[pltpu.VMEM(r.shape, r.dtype) for r in results]
        + [pltpu.SemaphoreType.DMA((len(results),))] * 2,
        compiler_params=pltpu.CompilerParams(vmem_limit_bytes=VMEM_LIMIT),
    )(*results)


def solution(mesh):
    placed = (
        P("req", None, None),
        P("req", None),
        P(),
        P(None, "head"),
        P(None, "head"),
        P(),
        P("head", None),
        P(),
        P("req", None, "head"),
        P("req", None),
        P("req", None),
        P("req"),
        P("req", None),
        P("req"),
    )
    return jax.shard_map(
        on_device,
        mesh=mesh,
        in_specs=placed,
        out_specs=(
            P("req", None, "head"),
            P("req", "head"),
            P("req", None, "head"),
            P("req", "head"),
        ),
        check_vma=False,
    )
```

```python
import functools

import jax
import jax.numpy as jnp
import numpy as np
from jax import lax
from jax.experimental import pallas as pl
from jax.experimental.pallas import tpu as pltpu
from jax.sharding import PartitionSpec as P

HEAD = 256
HALF = HEAD // 2
VMEM_LIMIT = 62 * 1024 * 1024
PAD = 16
SPAN = 256
eps_norm = 1e-06
rope_base = 1000000.0
neg_large = -1e30
MESH = pl.DeviceIdType.MESH


def rope_tables(longest):
    freq = rope_base ** (-2.0 * np.arange(HALF) / HEAD)
    low = np.arange(SPAN)[:, None] * freq[None, :]
    low = np.concatenate([np.cos(low), np.sin(low)], axis=1).astype(np.float32)
    coarse = low.astype(jnp.bfloat16)
    fine = (low - coarse.astype(np.float32)).astype(jnp.bfloat16)
    count = -(-(longest // SPAN + 1) // 8) * 8
    high = np.arange(count)[:, None] * float(SPAN) * freq[None, :]
    high = np.concatenate([np.cos(high), np.sin(high)], axis=1).astype(np.float32)
    return np.concatenate([coarse, fine], axis=1), high


def rms(values):
    return values * lax.rsqrt(jnp.mean(values * values, axis=-1, keepdims=True) + eps_norm)


def dot(a, b):
    return jnp.dot(a, b, preferred_element_type=jnp.float32)


def dot_t(a, b):
    return lax.dot_general(a, b, (((1,), (1,)), ((), ())), preferred_element_type=jnp.float32)


def kernel(
    n,
    outbound_h, page_table_h, cache_len_h, prompt_len_h, accepted_h,
    verify_h, prefill_x, attn_gain, w_query, w_keyval, qk_gain, w_out, post_gain,
    page_pool, table, high,
    verify_out, prefill_out, verify_kv, prefill_kv,
    outbound, page_table, cache_len, prompt_len, accepted, verify_x, table_row,
    x_v, vx_v, again_v, pgain_v, qkgain_v, table_v, high_v,
    wp_v, wo_v, pool_v, leaving, arrived, cached,
    normed, cos_v, sin_v, bias, kv_v, qv_v, attn_v, vattn_v,
    own_v, send_v, got_v, stat_v, gstat_v, vsend_v, vgot_v, out_v, vout_v, vkv_v,
    local_sem, page_send, page_recv, ex_send, ex_recv,
):
    me = lax.axis_index("req")
    side = lax.axis_index("head")
    rows, width = x_v.shape
    draft = verify_x.shape[1]
    half = width // 2
    heads = attn_v.shape[1] // HEAD
    pages = page_table.shape[1]
    pool_pages = pool_v.shape[0]
    page_rows = pool_v.shape[1]
    mine = pl.multiple_of(side * half, half)
    theirs = pl.multiple_of((1 - side) * half, half)

    barrier = pltpu.get_barrier_semaphore()
    pl.semaphore_signal(barrier, inc=1, device_id=(me, 1 - side), device_id_type=MESH)

    def greet(step, carry):
        pl.semaphore_signal(
            barrier, inc=1, device_id=(lax.rem(me + step, n), side), device_id_type=MESH
        )
        return carry

    lax.fori_loop(1, n, greet, 0)

    copies = []

    def fetch(src, dst):
        copy = pltpu.make_async_copy(src, dst, local_sem.at[len(copies)])
        copy.start()
        copies.append(copy)
        return copy

    put = fetch
    got_again = fetch(attn_gain, again_v)
    got_verify = fetch(verify_h, verify_x)
    got_x = fetch(prefill_x, x_v)
    got_outbound = fetch(outbound_h, outbound)
    got_small = [
        fetch(prompt_len_h, prompt_len),
        fetch(cache_len_h, cache_len),
        fetch(accepted_h, accepted),
        fetch(page_table_h, page_table),
        fetch(page_table_h, table_row),
    ]
    got_w = [fetch(w_keyval.at[:, pl.ds(i * HEAD, HEAD)], wp_v.at[i]) for i in range(2)]
    got_pool = fetch(page_pool, pool_v)
    got_table = fetch(table, table_v)
    got_high = fetch(high, high_v)
    got_qkgain = fetch(qk_gain, qkgain_v)
    got_w += [
        fetch(w_query.at[:, pl.ds(i * HEAD, HEAD)], wp_v.at[2 + i]) for i in range(heads)
    ]
    got_wo = [
        fetch(w_out.at[:, pl.ds(theirs, half)], wo_v.at[0]),
        fetch(w_out.at[:, pl.ds(mine, half)], wo_v.at[1]),
    ]
    got_pgain = fetch(post_gain, pgain_v)

    vx_v[...] = jnp.zeros_like(vx_v)
    got_verify.wait()
    got_again.wait()
    vx_v[0:draft, :] = verify_x[0].astype(jnp.float32)
    normed[rows:, :] = (rms(vx_v[...]) * again_v[...]).astype(jnp.bfloat16)

    got_x.wait()
    block = 16

    def norm_rows(i, carry):
        for u in range(4):
            at = pl.ds(pl.multiple_of(i * 4 * block, block) + u * block, block)
            normed[at, :] = (
                rms(x_v[at, :].astype(jnp.float32)) * again_v[...]
            ).astype(jnp.bfloat16)
        return carry

    lax.fori_loop(0, rows // (4 * block), norm_rows, 0)

    for copy in got_small:
        copy.wait()
    row = lax.broadcasted_iota(jnp.int32, (rows, 1), 0)
    start = jnp.zeros((rows, 1), jnp.int32)
    end = jnp.int32(0)
    for k in range(prompt_len.shape[1] - 1):
        end = end + prompt_len[0, k]
        start = jnp.where(row >= end, end, start)
    col = lax.broadcasted_iota(jnp.int32, (rows, rows), 1)
    bias[...] = jnp.where((col <= row) & (col >= start), 0.0, neg_large)
    length = cache_len[0, 0]
    vrow = lax.broadcasted_iota(jnp.int32, (PAD, 1), 0)
    vpos = length + jnp.minimum(vrow, draft - 1)
    lane = lax.broadcasted_iota(jnp.int32, (rows, SPAN), 1)
    vlane = lax.broadcasted_iota(jnp.int32, (PAD, SPAN), 1)
    got_table.wait()
    got_high.wait()
    got_qkgain.wait()

    def factors(pick):
        both = dot(jnp.where(pick, 1.0, 0.0).astype(jnp.bfloat16), table_v[...])
        return (
            both[:, :HALF] + both[:, HEAD:HEAD + HALF],
            both[:, HALF:HEAD] + both[:, HEAD + HALF:],
        )

    cos_p, sin_p = factors(lane == row - start)
    cos_v[0:rows, :] = cos_p
    sin_v[0:rows, :] = sin_p
    cos_l, sin_l = factors(vlane == jnp.bitwise_and(vpos, SPAN - 1))
    far = lax.shift_right_logical(vpos, 8)
    cos_h = jnp.zeros((PAD, HALF), jnp.float32)
    sin_h = jnp.zeros((PAD, HALF), jnp.float32)
    for k in range(high_v.shape[0]):
        cos_h = jnp.where(far == k, high_v[k:k + 1, :HALF], cos_h)
        sin_h = jnp.where(far == k, high_v[k:k + 1, HALF:], sin_h)
    cos_v[rows:, :] = cos_l * cos_h - sin_l * sin_h
    sin_v[rows:, :] = sin_l * cos_h + cos_l * sin_h

    def rope(values):
        first, second = values[:, :HALF], values[:, HALF:]
        cosine, sine = cos_v[...], sin_v[...]
        return jnp.concatenate(
            [first * cosine - second * sine, second * cosine + first * sine], axis=-1
        ).astype(jnp.bfloat16)

    got_w[0].wait()
    kv_v[:, :HEAD] = rope(rms(dot(normed[...], wp_v[0])) * qkgain_v[1:2, :])
    got_w[1].wait()
    kv_v[:, HEAD:] = rms(dot(normed[...], wp_v[1])).astype(jnp.bfloat16)
    put_kv = put(kv_v.at[pl.ds(0, rows)], prefill_kv)
    vkv = kv_v[rows:, :].astype(jnp.float32)
    vkv = jnp.where(vrow < accepted[0, 0], vkv, 0.0).astype(jnp.bfloat16)
    vkv_v[0] = vkv[0:draft, :]
    put_vkv = put(vkv_v, verify_kv)

    arrived[me] = jnp.zeros(arrived.shape[1:], arrived.dtype)
    got_outbound.wait()
    got_pool.wait()

    def pack(i, carry):
        for u in range(4):
            page = outbound[0, i * 4 + u]
            body = pool_v[jnp.clip(page, 0, pool_pages - 1)]
            leaving[i * 4 + u] = lax.select(page >= 0, body, jnp.zeros_like(body))
        return carry

    lax.fori_loop(0, n // 4, pack, 0)

    pl.semaphore_wait(barrier, n)

    def send(step, carry):
        d = lax.rem(me + step, n)
        pltpu.make_async_remote_copy(
            src_ref=leaving.at[d],
            dst_ref=arrived.at[me],
            send_sem=page_send.at[d],
            recv_sem=page_recv.at[me],
            device_id=(d, side),
            device_id_type=MESH,
        ).start()
        return carry

    lax.fori_loop(1, n, send, 0)

    for copy in got_w[2:]:
        copy.wait()

    def project(i):
        query = rope(rms(dot(normed[...], wp_v[2 + i])) * qkgain_v[0:1, :])
        qv_v[i * PAD:(i + 1) * PAD, :] = query[rows:, :]
        return query

    ahead = project(0)

    for i in range(heads):
        query = ahead
        if i + 1 < heads:
            ahead = project(i + 1)
        scores = dot_t(query[:rows, :], kv_v[:rows, :HEAD]) + bias[...]
        weights = jnp.exp(scores - jnp.max(scores, axis=-1, keepdims=True))
        share = 1.0 / jnp.sum(weights, axis=-1, keepdims=True)
        probs = (weights * share).astype(jnp.bfloat16)
        attn_v[:, i * HEAD:(i + 1) * HEAD] = dot(probs, kv_v[:rows, HEAD:]).astype(jnp.bfloat16)

    def swap(src, dst, k):
        copy = pltpu.make_async_remote_copy(
            src_ref=src,
            dst_ref=dst,
            send_sem=ex_send.at[k],
            recv_sem=ex_recv.at[k],
            device_id=(me, 1 - side),
            device_id_type=MESH,
        )
        copy.start()
        return copy

    got_wo[0].wait()
    send_v[...] = dot(attn_v[...], wo_v[0]).astype(send_v.dtype)
    swap_rows = swap(send_v, got_v, 0)
    got_wo[1].wait()
    own_v[...] = dot(attn_v[...], wo_v[1])

    group = 8

    def gather(i, carry):
        for u in range(group):
            page = page_table[0, i * group + u]
            at = pl.ds(pl.multiple_of(i * group * page_rows, page_rows) + u * page_rows, page_rows)
            cached[at, :] = pool_v[jnp.clip(page, 0, pool_pages - 1)]
        return carry

    lax.fori_loop(0, pages // group, gather, 0)
    square_row = lax.broadcasted_iota(jnp.int32, (pages, pages), 0)
    square_col = lax.broadcasted_iota(jnp.int32, (pages, pages), 1)
    spread = jnp.broadcast_to(table_row[...], (pages, pages))
    page_col = jnp.sum(
        jnp.where(square_row == square_col, spread, 0), axis=1, keepdims=True
    )
    slots = pages * page_rows
    slot_page = lax.broadcasted_iota(jnp.int32, (pages, slots), 0) * page_rows
    slot = lax.broadcasted_iota(jnp.int32, (pages, slots), 1)
    here = (slot >= slot_page) & (slot < slot_page + page_rows)
    here = here & (page_col < pool_pages) & (slot < length)
    here = jnp.sum(jnp.where(here, 1.0, 0.0), axis=0, keepdims=True)
    came = n * page_rows
    came_row = lax.broadcasted_iota(jnp.int32, (pages, came), 1)
    came_page = lax.shift_right_logical(came_row, page_rows.bit_length() - 1)
    came_slot = lax.broadcasted_iota(jnp.int32, (pages, came), 0) * page_rows
    came_slot = came_slot + came_row - came_page * page_rows
    uses = (page_col == came_page + pool_pages) & (came_slot < length)
    uses = jnp.sum(jnp.where(uses, 1.0, 0.0), axis=0, keepdims=True)

    swap_rows.wait()
    summed = own_v[...] + got_v[...].astype(jnp.float32)
    own_v[...] = summed
    stat_v[...] = jnp.broadcast_to(jnp.sum(summed * summed, axis=-1, keepdims=True), stat_v.shape)
    swap_stat = swap(stat_v, gstat_v, 1)

    queries = qv_v[...]
    old = jnp.where(here > 0.0, dot_t(queries, cached[:, :HEAD]), neg_large)
    new = dot_t(queries, kv_v[rows:, :HEAD])
    step = jnp.bitwise_and(lax.broadcasted_iota(jnp.int32, new.shape, 0), PAD - 1)
    new = jnp.where(lax.broadcasted_iota(jnp.int32, new.shape, 1) <= step, new, neg_large)
    peak = jnp.maximum(
        jnp.max(old, axis=-1, keepdims=True), jnp.max(new, axis=-1, keepdims=True)
    )
    old = jnp.exp(old - peak)
    new = jnp.exp(new - peak)
    total = jnp.sum(old, axis=-1, keepdims=True) + jnp.sum(new, axis=-1, keepdims=True)
    mixed = dot(old.astype(jnp.bfloat16), cached[:, HEAD:])
    mixed = mixed + dot(new.astype(jnp.bfloat16), kv_v[rows:, HEAD:])

    got_pgain.wait()
    gain = pgain_v[:, pl.ds(mine, half)]
    swap_stat.wait()
    square = stat_v[:, 0:1] + gstat_v[:, 0:1]
    scale = lax.rsqrt(square / width + eps_norm)
    out_v[...] = (
        x_v[:, pl.ds(mine, half)].astype(jnp.float32) + own_v[...] * scale * gain
    ).astype(out_v.dtype)
    put_out = put(out_v, prefill_out)

    def arrive(step, carry):
        s = lax.rem(me + n - step, n)
        pltpu.make_async_remote_copy(
            src_ref=leaving.at[s],
            dst_ref=arrived.at[s],
            send_sem=page_send.at[s],
            recv_sem=page_recv.at[s],
            device_id=(s, side),
            device_id_type=MESH,
        ).wait()
        return carry

    lax.fori_loop(1, n, arrive, 0)


    moved = arrived[...].reshape(came, 2 * HEAD)
    scores = jnp.where(uses > 0.0, dot_t(queries, moved[:, :HEAD]), neg_large)
    top = jnp.maximum(peak, jnp.max(scores, axis=-1, keepdims=True))
    weights = uses * jnp.exp(scores - top)
    keep = jnp.exp(peak - top)
    total = total * keep + jnp.sum(weights, axis=-1, keepdims=True)
    mixed = mixed * keep + dot(weights.astype(jnp.bfloat16), moved[:, HEAD:])
    mixed = (mixed * (1.0 / total)).astype(jnp.bfloat16)
    for i in range(heads):
        vattn_v[:, i * HEAD:(i + 1) * HEAD] = mixed[i * PAD:(i + 1) * PAD, :]

    vsend_v[0] = dot(vattn_v[...], wo_v[0])
    vsend_v[1] = dot(vattn_v[...], wo_v[1])
    swap_verify = swap(vsend_v, vgot_v, 2)

    swap_verify.wait()
    ours = vsend_v[1] + vgot_v[0]
    other = vsend_v[0] + vgot_v[1]
    square = jnp.sum(ours * ours, axis=-1, keepdims=True)
    square = square + jnp.sum(other * other, axis=-1, keepdims=True)
    final = vx_v[:, pl.ds(mine, half)] + ours * lax.rsqrt(square / width + eps_norm) * gain
    vout_v[0] = final[0:draft, :].astype(vout_v.dtype)
    put_vout = put(vout_v, verify_out)
    for copy in (put_kv, put_vkv, put_out, put_vout):
        copy.wait()


def write_out(count, *refs):
    sources, results, held = refs[:count], refs[count:2 * count], refs[2 * count:3 * count]
    in_sem, out_sem = refs[3 * count:]
    ins = [pltpu.make_async_copy(sources[k], held[k], in_sem.at[k]) for k in range(count)]
    outs = [pltpu.make_async_copy(held[k], results[k], out_sem.at[k]) for k in range(count)]
    for copy in ins:
        copy.start()
    for k in range(count):
        ins[k].wait()
        outs[k].start()
    for copy in outs:
        copy.wait()


def on_device(
    verify_x, prefill_x, attn_gain, w_query, w_keyval, qk_gain, w_out, post_gain,
    page_pool, outbound, page_table, cache_len, prompt_len, accepted,
):
    n = lax.axis_size("req")
    _, draft, width = verify_x.shape
    rows = prefill_x.shape[0]
    all_rows = rows + PAD
    columns = w_query.shape[1]
    heads = columns // HEAD
    half = width // 2
    pages = page_table.shape[1]
    page = page_pool.shape[1:]
    table, high = rope_tables(pages * page[0] + draft)
    bf16, f32 = jnp.bfloat16, jnp.float32
    hbm = pl.BlockSpec(memory_space=pltpu.HBM)
    moved = 22 + heads
    results = pl.pallas_call(
        functools.partial(kernel, n),
        out_shape=(
            jax.ShapeDtypeStruct((1, draft, half), bf16),
            jax.ShapeDtypeStruct((rows, half), bf16),
            jax.ShapeDtypeStruct((1, draft, 2 * HEAD), bf16),
            jax.ShapeDtypeStruct((rows, 2 * HEAD), bf16),
        ),
        in_specs=[hbm] * 16,
        out_specs=(hbm,) * 4,
        scratch_shapes=[
            pltpu.SMEM(outbound.shape, jnp.int32),
            pltpu.SMEM(page_table.shape, jnp.int32),
            pltpu.SMEM((1, 1), jnp.int32),
            pltpu.SMEM(prompt_len.shape, jnp.int32),
            pltpu.SMEM((1, 1), jnp.int32),
            pltpu.VMEM(verify_x.shape, bf16),
            pltpu.VMEM(page_table.shape, jnp.int32),
            pltpu.VMEM((rows, width), bf16),
            pltpu.VMEM((PAD, width), f32),
            pltpu.VMEM((1, width), f32),
            pltpu.VMEM((1, width), f32),
            pltpu.VMEM(qk_gain.shape, f32),
            pltpu.VMEM(table.shape, bf16),
            pltpu.VMEM(high.shape, f32),
            pltpu.VMEM((2 + heads, width, HEAD), bf16),
            pltpu.VMEM((2, columns, half), bf16),
            pltpu.VMEM(page_pool.shape, bf16),
            pltpu.VMEM((n,) + page, bf16),
            pltpu.VMEM((n,) + page, bf16),
            pltpu.VMEM((pages * page[0], page[1]), bf16),
            pltpu.VMEM((all_rows, width), bf16),
            pltpu.VMEM((all_rows, HALF), f32),
            pltpu.VMEM((all_rows, HALF), f32),
            pltpu.VMEM((rows, rows), f32),
            pltpu.VMEM((all_rows, 2 * HEAD), bf16),
            pltpu.VMEM((heads * PAD, HEAD), bf16),
            pltpu.VMEM((rows, columns), bf16),
            pltpu.VMEM((PAD, columns), bf16),
            pltpu.VMEM((rows, half), f32),
            pltpu.VMEM((rows, half), bf16),
            pltpu.VMEM((rows, half), bf16),
            pltpu.VMEM((rows, 128), f32),
            pltpu.VMEM((rows, 128), f32),
            pltpu.VMEM((2, PAD, half), f32),
            pltpu.VMEM((2, PAD, half), f32),
            pltpu.VMEM((rows, half), bf16),
            pltpu.VMEM((1, draft, half), bf16),
            pltpu.VMEM((1, draft, 2 * HEAD), bf16),
            pltpu.SemaphoreType.DMA((moved,)),
            pltpu.SemaphoreType.DMA((n,)),
            pltpu.SemaphoreType.DMA((n,)),
            pltpu.SemaphoreType.DMA((3,)),
            pltpu.SemaphoreType.DMA((3,)),
        ],
        compiler_params=pltpu.CompilerParams(
            collective_id=0, has_side_effects=True, vmem_limit_bytes=VMEM_LIMIT
        ),
        cost_estimate=pl.CostEstimate(
            flops=2 * all_rows * width * (2 * columns + 2 * HEAD),
            bytes_accessed=16 * 1024 * 1024,
            transcendentals=heads * rows * rows,
        ),
    )(
        outbound, page_table, cache_len[None], prompt_len, accepted[None],
        verify_x, prefill_x, attn_gain.reshape(1, -1), w_query, w_keyval, qk_gain, w_out,
        post_gain.reshape(1, -1), page_pool, jnp.asarray(table), jnp.asarray(high),
    )
    return pl.pallas_call(
        functools.partial(write_out, len(results)),
        out_shape=tuple(jax.ShapeDtypeStruct(r.shape, r.dtype) for r in results),
        in_specs=[pl.BlockSpec(memory_space=pl.ANY)] * 4,
        out_specs=(hbm,) * 4,
        scratch_shapes=[pltpu.VMEM(r.shape, r.dtype) for r in results]
        + [pltpu.SemaphoreType.DMA((len(results),))] * 2,
        compiler_params=pltpu.CompilerParams(vmem_limit_bytes=VMEM_LIMIT),
    )(*results)


def solution(mesh):
    placed = (
        P("req", None, None),
        P("req", None),
        P(),
        P(None, "head"),
        P(None, "head"),
        P(),
        P("head", None),
        P(),
        P("req", None, "head"),
        P("req", None),
        P("req", None),
        P("req"),
        P("req", None),
        P("req"),
    )
    return jax.shard_map(
        on_device,
        mesh=mesh,
        in_specs=placed,
        out_specs=(
            P("req", None, "head"),
            P("req", "head"),
            P("req", None, "head"),
            P("req", "head"),
        ),
        check_vma=False,
    )
```

```python
import functools

import jax
import jax.numpy as jnp
import numpy as np
from jax import lax
from jax.experimental import pallas as pl
from jax.experimental.pallas import tpu as pltpu
from jax.sharding import PartitionSpec as P

HEAD = 256
HALF = HEAD // 2
VMEM_LIMIT = 62 * 1024 * 1024
PAD = 16
SPAN = 256
eps_norm = 1e-06
rope_base = 1000000.0
neg_large = -1e30
MESH = pl.DeviceIdType.MESH


def rope_tables(longest):
    freq = rope_base ** (-2.0 * np.arange(HALF) / HEAD)
    low = np.arange(SPAN)[:, None] * freq[None, :]
    low = np.concatenate([np.cos(low), np.sin(low)], axis=1).astype(np.float32)
    coarse = low.astype(jnp.bfloat16)
    fine = (low - coarse.astype(np.float32)).astype(jnp.bfloat16)
    count = -(-(longest // SPAN + 1) // 8) * 8
    high = np.arange(count)[:, None] * float(SPAN) * freq[None, :]
    high = np.concatenate([np.cos(high), np.sin(high)], axis=1).astype(np.float32)
    return np.concatenate([coarse, fine], axis=1), high


def rms(values):
    return values * lax.rsqrt(jnp.mean(values * values, axis=-1, keepdims=True) + eps_norm)


def dot(a, b):
    return jnp.dot(a, b, preferred_element_type=jnp.float32)


def dot_t(a, b):
    return lax.dot_general(a, b, (((1,), (1,)), ((), ())), preferred_element_type=jnp.float32)


def kernel(
    n,
    outbound_h, page_table_h, cache_len_h, prompt_len_h, accepted_h,
    verify_h, prefill_x, attn_gain, w_query, w_keyval, qk_gain, w_out, post_gain,
    page_pool, table, high,
    verify_out, prefill_out, verify_kv, prefill_kv,
    outbound, page_table, cache_len, prompt_len, accepted, verify_x, table_row,
    x_v, vx_v, again_v, pgain_v, qkgain_v, table_v, high_v,
    wp_v, wo_v, pool_v, leaving, arrived, cached,
    normed, cos_v, sin_v, bias, kv_v, qv_v, attn_v, vattn_v,
    own_v, send_v, got_v, stat_v, gstat_v, vsend_v, vgot_v, out_v, vout_v, vkv_v,
    local_sem, page_send, page_recv, ex_send, ex_recv,
):
    me = lax.axis_index("req")
    side = lax.axis_index("head")
    rows, width = x_v.shape
    draft = verify_x.shape[1]
    half = width // 2
    heads = attn_v.shape[1] // HEAD
    pages = page_table.shape[1]
    pool_pages = pool_v.shape[0]
    page_rows = pool_v.shape[1]
    mine = pl.multiple_of(side * half, half)
    theirs = pl.multiple_of((1 - side) * half, half)

    copies = []

    def fetch(src, dst):
        copy = pltpu.make_async_copy(src, dst, local_sem.at[len(copies)])
        copy.start()
        copies.append(copy)
        return copy

    put = fetch
    got_again = fetch(attn_gain, again_v)
    got_verify = fetch(verify_h, verify_x)
    got_x = fetch(prefill_x, x_v)
    got_outbound = fetch(outbound_h, outbound)
    got_pool = fetch(page_pool, pool_v)

    barrier = pltpu.get_barrier_semaphore()
    pl.semaphore_signal(barrier, inc=1, device_id=(me, 1 - side), device_id_type=MESH)

    def greet(step, carry):
        pl.semaphore_signal(
            barrier, inc=1, device_id=(lax.rem(me + step, n), side), device_id_type=MESH
        )
        return carry

    lax.fori_loop(1, n, greet, 0)

    got_small = [
        fetch(prompt_len_h, prompt_len),
        fetch(cache_len_h, cache_len),
        fetch(accepted_h, accepted),
        fetch(page_table_h, page_table),
        fetch(page_table_h, table_row),
    ]
    got_w = [fetch(w_keyval.at[:, pl.ds(i * HEAD, HEAD)], wp_v.at[i]) for i in range(2)]
    got_table = fetch(table, table_v)
    got_high = fetch(high, high_v)
    got_qkgain = fetch(qk_gain, qkgain_v)
    got_w += [
        fetch(w_query.at[:, pl.ds(i * HEAD, HEAD)], wp_v.at[2 + i]) for i in range(heads)
    ]
    got_wo = [
        fetch(w_out.at[:, pl.ds(theirs, half)], wo_v.at[0]),
        fetch(w_out.at[:, pl.ds(mine, half)], wo_v.at[1]),
    ]
    got_pgain = fetch(post_gain, pgain_v)

    vx_v[...] = jnp.zeros_like(vx_v)
    got_verify.wait()
    got_again.wait()
    vx_v[0:draft, :] = verify_x[0].astype(jnp.float32)
    normed[rows:, :] = (rms(vx_v[...]) * again_v[...]).astype(jnp.bfloat16)

    got_x.wait()
    block = 16

    def norm_rows(i, carry):
        for u in range(4):
            at = pl.ds(pl.multiple_of(i * 4 * block, block) + u * block, block)
            normed[at, :] = (
                rms(x_v[at, :].astype(jnp.float32)) * again_v[...]
            ).astype(jnp.bfloat16)
        return carry

    lax.fori_loop(0, rows // (4 * block), norm_rows, 0)

    arrived[me] = jnp.zeros(arrived.shape[1:], arrived.dtype)
    got_outbound.wait()
    got_pool.wait()

    def pack(i, carry):
        for u in range(4):
            page = outbound[0, i * 4 + u]
            body = pool_v[jnp.clip(page, 0, pool_pages - 1)]
            leaving[i * 4 + u] = lax.select(page >= 0, body, jnp.zeros_like(body))
        return carry

    lax.fori_loop(0, n // 4, pack, 0)

    pl.semaphore_wait(barrier, n)

    def send(step, carry):
        d = lax.rem(me + step, n)
        pltpu.make_async_remote_copy(
            src_ref=leaving.at[d],
            dst_ref=arrived.at[me],
            send_sem=page_send.at[d],
            recv_sem=page_recv.at[me],
            device_id=(d, side),
            device_id_type=MESH,
        ).start()
        return carry

    lax.fori_loop(1, n, send, 0)

    for copy in got_small:
        copy.wait()
    row = lax.broadcasted_iota(jnp.int32, (rows, 1), 0)
    start = jnp.zeros((rows, 1), jnp.int32)
    end = jnp.int32(0)
    for k in range(prompt_len.shape[1] - 1):
        end = end + prompt_len[0, k]
        start = jnp.where(row >= end, end, start)
    col = lax.broadcasted_iota(jnp.int32, (rows, rows), 1)
    bias[...] = jnp.where((col <= row) & (col >= start), 0.0, neg_large)
    length = cache_len[0, 0]
    vrow = lax.broadcasted_iota(jnp.int32, (PAD, 1), 0)
    vpos = length + jnp.minimum(vrow, draft - 1)
    lane = lax.broadcasted_iota(jnp.int32, (rows, SPAN), 1)
    vlane = lax.broadcasted_iota(jnp.int32, (PAD, SPAN), 1)
    got_table.wait()
    got_high.wait()
    got_qkgain.wait()

    def factors(pick):
        both = dot(jnp.where(pick, 1.0, 0.0).astype(jnp.bfloat16), table_v[...])
        return (
            both[:, :HALF] + both[:, HEAD:HEAD + HALF],
            both[:, HALF:HEAD] + both[:, HEAD + HALF:],
        )

    cos_p, sin_p = factors(lane == row - start)
    cos_v[0:rows, :] = cos_p
    sin_v[0:rows, :] = sin_p
    cos_l, sin_l = factors(vlane == jnp.bitwise_and(vpos, SPAN - 1))
    far = lax.shift_right_logical(vpos, 8)
    cos_h = jnp.zeros((PAD, HALF), jnp.float32)
    sin_h = jnp.zeros((PAD, HALF), jnp.float32)
    for k in range(high_v.shape[0]):
        cos_h = jnp.where(far == k, high_v[k:k + 1, :HALF], cos_h)
        sin_h = jnp.where(far == k, high_v[k:k + 1, HALF:], sin_h)
    cos_v[rows:, :] = cos_l * cos_h - sin_l * sin_h
    sin_v[rows:, :] = sin_l * cos_h + cos_l * sin_h

    def rope(values):
        first, second = values[:, :HALF], values[:, HALF:]
        cosine, sine = cos_v[...], sin_v[...]
        return jnp.concatenate(
            [first * cosine - second * sine, second * cosine + first * sine], axis=-1
        ).astype(jnp.bfloat16)

    got_w[0].wait()
    kv_v[:, :HEAD] = rope(rms(dot(normed[...], wp_v[0])) * qkgain_v[1:2, :])
    got_w[1].wait()
    kv_v[:, HEAD:] = rms(dot(normed[...], wp_v[1])).astype(jnp.bfloat16)
    put_kv = put(kv_v.at[pl.ds(0, rows)], prefill_kv)
    vkv = kv_v[rows:, :].astype(jnp.float32)
    vkv = jnp.where(vrow < accepted[0, 0], vkv, 0.0).astype(jnp.bfloat16)
    vkv_v[0] = vkv[0:draft, :]
    put_vkv = put(vkv_v, verify_kv)

    for copy in got_w[2:]:
        copy.wait()

    def project(i):
        query = rope(rms(dot(normed[...], wp_v[2 + i])) * qkgain_v[0:1, :])
        qv_v[i * PAD:(i + 1) * PAD, :] = query[rows:, :]
        return query

    ahead = project(0)

    for i in range(heads):
        query = ahead
        if i + 1 < heads:
            ahead = project(i + 1)
        scores = dot_t(query[:rows, :], kv_v[:rows, :HEAD]) + bias[...]
        weights = jnp.exp(scores - jnp.max(scores, axis=-1, keepdims=True))
        share = 1.0 / jnp.sum(weights, axis=-1, keepdims=True)
        probs = (weights * share).astype(jnp.bfloat16)
        attn_v[:, i * HEAD:(i + 1) * HEAD] = dot(probs, kv_v[:rows, HEAD:]).astype(jnp.bfloat16)

    def swap(src, dst, k):
        copy = pltpu.make_async_remote_copy(
            src_ref=src,
            dst_ref=dst,
            send_sem=ex_send.at[k],
            recv_sem=ex_recv.at[k],
            device_id=(me, 1 - side),
            device_id_type=MESH,
        )
        copy.start()
        return copy

    got_wo[0].wait()
    send_v[...] = dot(attn_v[...], wo_v[0]).astype(send_v.dtype)
    swap_rows = swap(send_v, got_v, 0)
    got_wo[1].wait()
    own_v[...] = dot(attn_v[...], wo_v[1])

    group = 8

    def gather(i, carry):
        for u in range(group):
            page = page_table[0, i * group + u]
            at = pl.ds(pl.multiple_of(i * group * page_rows, page_rows) + u * page_rows, page_rows)
            cached[at, :] = pool_v[jnp.clip(page, 0, pool_pages - 1)]
        return carry

    lax.fori_loop(0, pages // group, gather, 0)
    square_row = lax.broadcasted_iota(jnp.int32, (pages, pages), 0)
    square_col = lax.broadcasted_iota(jnp.int32, (pages, pages), 1)
    spread = jnp.broadcast_to(table_row[...], (pages, pages))
    page_col = jnp.sum(
        jnp.where(square_row == square_col, spread, 0), axis=1, keepdims=True
    )
    slots = pages * page_rows
    slot_page = lax.broadcasted_iota(jnp.int32, (pages, slots), 0) * page_rows
    slot = lax.broadcasted_iota(jnp.int32, (pages, slots), 1)
    here = (slot >= slot_page) & (slot < slot_page + page_rows)
    here = here & (page_col < pool_pages) & (slot < length)
    here = jnp.sum(jnp.where(here, 1.0, 0.0), axis=0, keepdims=True)
    came = n * page_rows
    came_row = lax.broadcasted_iota(jnp.int32, (pages, came), 1)
    came_page = lax.shift_right_logical(came_row, page_rows.bit_length() - 1)
    came_slot = lax.broadcasted_iota(jnp.int32, (pages, came), 0) * page_rows
    came_slot = came_slot + came_row - came_page * page_rows
    uses = (page_col == came_page + pool_pages) & (came_slot < length)
    uses = jnp.sum(jnp.where(uses, 1.0, 0.0), axis=0, keepdims=True)

    swap_rows.wait()
    summed = own_v[...] + got_v[...].astype(jnp.float32)
    own_v[...] = summed
    stat_v[...] = jnp.broadcast_to(jnp.sum(summed * summed, axis=-1, keepdims=True), stat_v.shape)
    swap_stat = swap(stat_v, gstat_v, 1)

    queries = qv_v[...]
    old = jnp.where(here > 0.0, dot_t(queries, cached[:, :HEAD]), neg_large)
    new = dot_t(queries, kv_v[rows:, :HEAD])
    step = jnp.bitwise_and(lax.broadcasted_iota(jnp.int32, new.shape, 0), PAD - 1)
    new = jnp.where(lax.broadcasted_iota(jnp.int32, new.shape, 1) <= step, new, neg_large)
    peak = jnp.maximum(
        jnp.max(old, axis=-1, keepdims=True), jnp.max(new, axis=-1, keepdims=True)
    )
    old = jnp.exp(old - peak)
    new = jnp.exp(new - peak)
    total = jnp.sum(old, axis=-1, keepdims=True) + jnp.sum(new, axis=-1, keepdims=True)
    mixed = dot(old.astype(jnp.bfloat16), cached[:, HEAD:])
    mixed = mixed + dot(new.astype(jnp.bfloat16), kv_v[rows:, HEAD:])

    got_pgain.wait()
    gain = pgain_v[:, pl.ds(mine, half)]
    swap_stat.wait()
    square = stat_v[:, 0:1] + gstat_v[:, 0:1]
    scale = lax.rsqrt(square / width + eps_norm)
    out_v[...] = (
        x_v[:, pl.ds(mine, half)].astype(jnp.float32) + own_v[...] * scale * gain
    ).astype(out_v.dtype)
    put_out = put(out_v, prefill_out)

    def arrive(step, carry):
        s = lax.rem(me + n - step, n)
        pltpu.make_async_remote_copy(
            src_ref=leaving.at[s],
            dst_ref=arrived.at[s],
            send_sem=page_send.at[s],
            recv_sem=page_recv.at[s],
            device_id=(s, side),
            device_id_type=MESH,
        ).wait()
        return carry

    lax.fori_loop(1, n, arrive, 0)


    moved = arrived[...].reshape(came, 2 * HEAD)
    scores = jnp.where(uses > 0.0, dot_t(queries, moved[:, :HEAD]), neg_large)
    top = jnp.maximum(peak, jnp.max(scores, axis=-1, keepdims=True))
    weights = uses * jnp.exp(scores - top)
    keep = jnp.exp(peak - top)
    total = total * keep + jnp.sum(weights, axis=-1, keepdims=True)
    mixed = mixed * keep + dot(weights.astype(jnp.bfloat16), moved[:, HEAD:])
    mixed = (mixed * (1.0 / total)).astype(jnp.bfloat16)
    for i in range(heads):
        vattn_v[:, i * HEAD:(i + 1) * HEAD] = mixed[i * PAD:(i + 1) * PAD, :]

    vsend_v[0] = dot(vattn_v[...], wo_v[0])
    vsend_v[1] = dot(vattn_v[...], wo_v[1])
    swap_verify = swap(vsend_v, vgot_v, 2)

    swap_verify.wait()
    ours = vsend_v[1] + vgot_v[0]
    other = vsend_v[0] + vgot_v[1]
    square = jnp.sum(ours * ours, axis=-1, keepdims=True)
    square = square + jnp.sum(other * other, axis=-1, keepdims=True)
    final = vx_v[:, pl.ds(mine, half)] + ours * lax.rsqrt(square / width + eps_norm) * gain
    vout_v[0] = final[0:draft, :].astype(vout_v.dtype)
    put_vout = put(vout_v, verify_out)
    for copy in (put_kv, put_vkv, put_out, put_vout):
        copy.wait()


def write_out(count, *refs):
    sources, results, held = refs[:count], refs[count:2 * count], refs[2 * count:3 * count]
    in_sem, out_sem = refs[3 * count:]
    ins = [pltpu.make_async_copy(sources[k], held[k], in_sem.at[k]) for k in range(count)]
    outs = [pltpu.make_async_copy(held[k], results[k], out_sem.at[k]) for k in range(count)]
    for copy in ins:
        copy.start()
    for k in range(count):
        ins[k].wait()
        outs[k].start()
    for copy in outs:
        copy.wait()


def on_device(
    verify_x, prefill_x, attn_gain, w_query, w_keyval, qk_gain, w_out, post_gain,
    page_pool, outbound, page_table, cache_len, prompt_len, accepted,
):
    n = lax.axis_size("req")
    _, draft, width = verify_x.shape
    rows = prefill_x.shape[0]
    all_rows = rows + PAD
    columns = w_query.shape[1]
    heads = columns // HEAD
    half = width // 2
    pages = page_table.shape[1]
    page = page_pool.shape[1:]
    table, high = rope_tables(pages * page[0] + draft)
    bf16, f32 = jnp.bfloat16, jnp.float32
    hbm = pl.BlockSpec(memory_space=pltpu.HBM)
    moved = 22 + heads
    results = pl.pallas_call(
        functools.partial(kernel, n),
        out_shape=(
            jax.ShapeDtypeStruct((1, draft, half), bf16),
            jax.ShapeDtypeStruct((rows, half), bf16),
            jax.ShapeDtypeStruct((1, draft, 2 * HEAD), bf16),
            jax.ShapeDtypeStruct((rows, 2 * HEAD), bf16),
        ),
        in_specs=[hbm] * 16,
        out_specs=(hbm,) * 4,
        scratch_shapes=[
            pltpu.SMEM(outbound.shape, jnp.int32),
            pltpu.SMEM(page_table.shape, jnp.int32),
            pltpu.SMEM((1, 1), jnp.int32),
            pltpu.SMEM(prompt_len.shape, jnp.int32),
            pltpu.SMEM((1, 1), jnp.int32),
            pltpu.VMEM(verify_x.shape, bf16),
            pltpu.VMEM(page_table.shape, jnp.int32),
            pltpu.VMEM((rows, width), bf16),
            pltpu.VMEM((PAD, width), f32),
            pltpu.VMEM((1, width), f32),
            pltpu.VMEM((1, width), f32),
            pltpu.VMEM(qk_gain.shape, f32),
            pltpu.VMEM(table.shape, bf16),
            pltpu.VMEM(high.shape, f32),
            pltpu.VMEM((2 + heads, width, HEAD), bf16),
            pltpu.VMEM((2, columns, half), bf16),
            pltpu.VMEM(page_pool.shape, bf16),
            pltpu.VMEM((n,) + page, bf16),
            pltpu.VMEM((n,) + page, bf16),
            pltpu.VMEM((pages * page[0], page[1]), bf16),
            pltpu.VMEM((all_rows, width), bf16),
            pltpu.VMEM((all_rows, HALF), f32),
            pltpu.VMEM((all_rows, HALF), f32),
            pltpu.VMEM((rows, rows), f32),
            pltpu.VMEM((all_rows, 2 * HEAD), bf16),
            pltpu.VMEM((heads * PAD, HEAD), bf16),
            pltpu.VMEM((rows, columns), bf16),
            pltpu.VMEM((PAD, columns), bf16),
            pltpu.VMEM((rows, half), f32),
            pltpu.VMEM((rows, half), bf16),
            pltpu.VMEM((rows, half), bf16),
            pltpu.VMEM((rows, 128), f32),
            pltpu.VMEM((rows, 128), f32),
            pltpu.VMEM((2, PAD, half), f32),
            pltpu.VMEM((2, PAD, half), f32),
            pltpu.VMEM((rows, half), bf16),
            pltpu.VMEM((1, draft, half), bf16),
            pltpu.VMEM((1, draft, 2 * HEAD), bf16),
            pltpu.SemaphoreType.DMA((moved,)),
            pltpu.SemaphoreType.DMA((n,)),
            pltpu.SemaphoreType.DMA((n,)),
            pltpu.SemaphoreType.DMA((3,)),
            pltpu.SemaphoreType.DMA((3,)),
        ],
        compiler_params=pltpu.CompilerParams(
            collective_id=0, has_side_effects=True, vmem_limit_bytes=VMEM_LIMIT
        ),
        cost_estimate=pl.CostEstimate(
            flops=2 * all_rows * width * (2 * columns + 2 * HEAD),
            bytes_accessed=16 * 1024 * 1024,
            transcendentals=heads * rows * rows,
        ),
    )(
        outbound, page_table, cache_len[None], prompt_len, accepted[None],
        verify_x, prefill_x, attn_gain.reshape(1, -1), w_query, w_keyval, qk_gain, w_out,
        post_gain.reshape(1, -1), page_pool, jnp.asarray(table), jnp.asarray(high),
    )
    return pl.pallas_call(
        functools.partial(write_out, len(results)),
        out_shape=tuple(jax.ShapeDtypeStruct(r.shape, r.dtype) for r in results),
        in_specs=[pl.BlockSpec(memory_space=pl.ANY)] * 4,
        out_specs=(hbm,) * 4,
        scratch_shapes=[pltpu.VMEM(r.shape, r.dtype) for r in results]
        + [pltpu.SemaphoreType.DMA((len(results),))] * 2,
        compiler_params=pltpu.CompilerParams(vmem_limit_bytes=VMEM_LIMIT),
    )(*results)


def solution(mesh):
    placed = (
        P("req", None, None),
        P("req", None),
        P(),
        P(None, "head"),
        P(None, "head"),
        P(),
        P("head", None),
        P(),
        P("req", None, "head"),
        P("req", None),
        P("req", None),
        P("req"),
        P("req", None),
        P("req"),
    )
    return jax.shard_map(
        on_device,
        mesh=mesh,
        in_specs=placed,
        out_specs=(
            P("req", None, "head"),
            P("req", "head"),
            P("req", None, "head"),
            P("req", "head"),
        ),
        check_vma=False,
    )
```

```python
import functools

import jax
import jax.numpy as jnp
import numpy as np
from jax import lax
from jax.experimental import pallas as pl
from jax.experimental.pallas import tpu as pltpu
from jax.sharding import PartitionSpec as P

HEAD = 256
HALF = HEAD // 2
VMEM_LIMIT = 62 * 1024 * 1024
PAD = 16
SPAN = 256
eps_norm = 1e-06
rope_base = 1000000.0
neg_large = -1e30
MESH = pl.DeviceIdType.MESH


def rope_tables(longest):
    freq = rope_base ** (-2.0 * np.arange(HALF) / HEAD)
    low = np.arange(SPAN)[:, None] * freq[None, :]
    low = np.concatenate([np.cos(low), np.sin(low)], axis=1).astype(np.float32)
    coarse = low.astype(jnp.bfloat16)
    fine = (low - coarse.astype(np.float32)).astype(jnp.bfloat16)
    count = -(-(longest // SPAN + 1) // 8) * 8
    high = np.arange(count)[:, None] * float(SPAN) * freq[None, :]
    high = np.concatenate([np.cos(high), np.sin(high)], axis=1).astype(np.float32)
    return np.concatenate([coarse, fine], axis=1), high


def rms(values):
    return values * lax.rsqrt(jnp.mean(values * values, axis=-1, keepdims=True) + eps_norm)


def dot(a, b):
    return jnp.dot(a, b, preferred_element_type=jnp.float32)


def dot_t(a, b):
    return lax.dot_general(a, b, (((1,), (1,)), ((), ())), preferred_element_type=jnp.float32)


def kernel(
    n,
    outbound_h, page_table_h, cache_len_h, prompt_len_h, accepted_h,
    verify_h, prefill_x, attn_gain, w_query, w_keyval, qk_gain, w_out, post_gain,
    page_pool, table, high,
    verify_out, prefill_out, verify_kv, prefill_kv,
    outbound, page_table, cache_len, prompt_len, accepted, verify_x, table_row,
    x_v, vx_v, again_v, pgain_v, qkgain_v, table_v, high_v,
    wp_v, wo_v, pool_v, leaving, arrived, cached,
    normed, cos_v, sin_v, bias, kv_v, qv_v, attn_v, vattn_v,
    own_v, send_v, got_v, stat_v, gstat_v, vsend_v, vgot_v, out_v, vout_v, vkv_v,
    local_sem, page_send, page_recv, ex_send, ex_recv,
):
    me = lax.axis_index("req")
    side = lax.axis_index("head")
    rows, width = x_v.shape
    draft = verify_x.shape[1]
    half = width // 2
    heads = attn_v.shape[1] // HEAD
    pages = page_table.shape[1]
    pool_pages = pool_v.shape[0]
    page_rows = pool_v.shape[1]
    mine = pl.multiple_of(side * half, half)
    theirs = pl.multiple_of((1 - side) * half, half)

    barrier = pltpu.get_barrier_semaphore()
    pl.semaphore_signal(barrier, inc=1, device_id=(me, 1 - side), device_id_type=MESH)

    def greet(step, carry):
        pl.semaphore_signal(
            barrier, inc=1, device_id=(lax.rem(me + step, n), side), device_id_type=MESH
        )
        return carry

    lax.fori_loop(1, n, greet, 0)

    copies = []

    def fetch(src, dst):
        copy = pltpu.make_async_copy(src, dst, local_sem.at[len(copies)])
        copy.start()
        copies.append(copy)
        return copy

    put = fetch
    got_again = fetch(attn_gain, again_v)
    got_verify = fetch(verify_h, verify_x)
    got_x = fetch(prefill_x, x_v)
    got_outbound = fetch(outbound_h, outbound)
    got_small = [
        fetch(prompt_len_h, prompt_len),
        fetch(cache_len_h, cache_len),
        fetch(accepted_h, accepted),
        fetch(page_table_h, page_table),
        fetch(page_table_h, table_row),
    ]
    got_w = [fetch(w_keyval.at[:, pl.ds(i * HEAD, HEAD)], wp_v.at[i]) for i in range(2)]
    got_pool = fetch(page_pool, pool_v)
    got_table = fetch(table, table_v)
    got_high = fetch(high, high_v)
    got_qkgain = fetch(qk_gain, qkgain_v)
    got_w += [
        fetch(w_query.at[:, pl.ds(i * HEAD, HEAD)], wp_v.at[2 + i]) for i in range(heads)
    ]
    got_wo = [
        fetch(w_out.at[:, pl.ds(theirs, half)], wo_v.at[0]),
        fetch(w_out.at[:, pl.ds(mine, half)], wo_v.at[1]),
    ]
    got_pgain = fetch(post_gain, pgain_v)

    vx_v[...] = jnp.zeros_like(vx_v)
    got_verify.wait()
    got_again.wait()
    vx_v[0:draft, :] = verify_x[0].astype(jnp.float32)
    normed[rows:, :] = (rms(vx_v[...]) * again_v[...]).astype(jnp.bfloat16)

    got_x.wait()
    block = 16

    def norm_rows(i, carry):
        for u in range(4):
            at = pl.ds(pl.multiple_of(i * 4 * block, block) + u * block, block)
            normed[at, :] = (
                rms(x_v[at, :].astype(jnp.float32)) * again_v[...]
            ).astype(jnp.bfloat16)
        return carry

    lax.fori_loop(0, rows // (4 * block), norm_rows, 0)

    for copy in got_small:
        copy.wait()
    row = lax.broadcasted_iota(jnp.int32, (rows, 1), 0)
    start = jnp.zeros((rows, 1), jnp.int32)
    end = jnp.int32(0)
    for k in range(prompt_len.shape[1] - 1):
        end = end + prompt_len[0, k]
        start = jnp.where(row >= end, end, start)
    col = lax.broadcasted_iota(jnp.int32, (rows, rows), 1)
    bias[...] = jnp.where((col <= row) & (col >= start), 0.0, neg_large)
    length = cache_len[0, 0]
    vrow = lax.broadcasted_iota(jnp.int32, (PAD, 1), 0)
    vpos = length + jnp.minimum(vrow, draft - 1)
    lane = lax.broadcasted_iota(jnp.int32, (rows, SPAN), 1)
    vlane = lax.broadcasted_iota(jnp.int32, (PAD, SPAN), 1)
    got_table.wait()
    got_high.wait()
    got_qkgain.wait()

    def factors(pick):
        both = dot(jnp.where(pick, 1.0, 0.0).astype(jnp.bfloat16), table_v[...])
        return (
            both[:, :HALF] + both[:, HEAD:HEAD + HALF],
            both[:, HALF:HEAD] + both[:, HEAD + HALF:],
        )

    cos_p, sin_p = factors(lane == row - start)
    cos_v[0:rows, :] = cos_p
    sin_v[0:rows, :] = sin_p
    cos_l, sin_l = factors(vlane == jnp.bitwise_and(vpos, SPAN - 1))
    far = lax.shift_right_logical(vpos, 8)
    cos_h = jnp.zeros((PAD, HALF), jnp.float32)
    sin_h = jnp.zeros((PAD, HALF), jnp.float32)
    for k in range(high_v.shape[0]):
        cos_h = jnp.where(far == k, high_v[k:k + 1, :HALF], cos_h)
        sin_h = jnp.where(far == k, high_v[k:k + 1, HALF:], sin_h)
    cos_v[rows:, :] = cos_l * cos_h - sin_l * sin_h
    sin_v[rows:, :] = sin_l * cos_h + cos_l * sin_h

    def rope(values):
        first, second = values[:, :HALF], values[:, HALF:]
        cosine, sine = cos_v[...], sin_v[...]
        return jnp.concatenate(
            [first * cosine - second * sine, second * cosine + first * sine], axis=-1
        ).astype(jnp.bfloat16)

    got_w[0].wait()
    kv_v[:, :HEAD] = rope(rms(dot(normed[...], wp_v[0])) * qkgain_v[1:2, :])
    arrived[me] = jnp.zeros(arrived.shape[1:], arrived.dtype)
    got_outbound.wait()
    got_pool.wait()

    def pack(i, carry):
        for u in range(4):
            page = outbound[0, i * 4 + u]
            body = pool_v[jnp.clip(page, 0, pool_pages - 1)]
            leaving[i * 4 + u] = lax.select(page >= 0, body, jnp.zeros_like(body))
        return carry

    lax.fori_loop(0, n // 4, pack, 0)

    pl.semaphore_wait(barrier, n)

    def send(step, carry):
        turn = n // 2 + (step // 2) * (1 - 2 * (step % 2))
        d = lax.rem(me + turn, n)
        pltpu.make_async_remote_copy(
            src_ref=leaving.at[d],
            dst_ref=arrived.at[me],
            send_sem=page_send.at[d],
            recv_sem=page_recv.at[me],
            device_id=(d, side),
            device_id_type=MESH,
        ).start()
        return carry

    lax.fori_loop(1, n, send, 0)

    got_w[1].wait()
    kv_v[:, HEAD:] = rms(dot(normed[...], wp_v[1])).astype(jnp.bfloat16)
    put_kv = put(kv_v.at[pl.ds(0, rows)], prefill_kv)
    vkv = kv_v[rows:, :].astype(jnp.float32)
    vkv = jnp.where(vrow < accepted[0, 0], vkv, 0.0).astype(jnp.bfloat16)
    vkv_v[0] = vkv[0:draft, :]
    put_vkv = put(vkv_v, verify_kv)

    for copy in got_w[2:]:
        copy.wait()

    def project(i):
        query = rope(rms(dot(normed[...], wp_v[2 + i])) * qkgain_v[0:1, :])
        qv_v[i * PAD:(i + 1) * PAD, :] = query[rows:, :]
        return query

    ahead = project(0)

    for i in range(heads):
        query = ahead
        if i + 1 < heads:
            ahead = project(i + 1)
        scores = dot_t(query[:rows, :], kv_v[:rows, :HEAD]) + bias[...]
        weights = jnp.exp(scores - jnp.max(scores, axis=-1, keepdims=True))
        share = 1.0 / jnp.sum(weights, axis=-1, keepdims=True)
        probs = (weights * share).astype(jnp.bfloat16)
        attn_v[:, i * HEAD:(i + 1) * HEAD] = dot(probs, kv_v[:rows, HEAD:]).astype(jnp.bfloat16)

    def swap(src, dst, k):
        copy = pltpu.make_async_remote_copy(
            src_ref=src,
            dst_ref=dst,
            send_sem=ex_send.at[k],
            recv_sem=ex_recv.at[k],
            device_id=(me, 1 - side),
            device_id_type=MESH,
        )
        copy.start()
        return copy

    got_wo[0].wait()
    send_v[...] = dot(attn_v[...], wo_v[0]).astype(send_v.dtype)
    swap_rows = swap(send_v, got_v, 0)
    got_wo[1].wait()
    own_v[...] = dot(attn_v[...], wo_v[1])

    group = 8

    def gather(i, carry):
        for u in range(group):
            page = page_table[0, i * group + u]
            at = pl.ds(pl.multiple_of(i * group * page_rows, page_rows) + u * page_rows, page_rows)
            cached[at, :] = pool_v[jnp.clip(page, 0, pool_pages - 1)]
        return carry

    lax.fori_loop(0, pages // group, gather, 0)
    square_row = lax.broadcasted_iota(jnp.int32, (pages, pages), 0)
    square_col = lax.broadcasted_iota(jnp.int32, (pages, pages), 1)
    spread = jnp.broadcast_to(table_row[...], (pages, pages))
    page_col = jnp.sum(
        jnp.where(square_row == square_col, spread, 0), axis=1, keepdims=True
    )
    slots = pages * page_rows
    slot_page = lax.broadcasted_iota(jnp.int32, (pages, slots), 0) * page_rows
    slot = lax.broadcasted_iota(jnp.int32, (pages, slots), 1)
    here = (slot >= slot_page) & (slot < slot_page + page_rows)
    here = here & (page_col < pool_pages) & (slot < length)
    here = jnp.sum(jnp.where(here, 1.0, 0.0), axis=0, keepdims=True)
    came = n * page_rows
    came_row = lax.broadcasted_iota(jnp.int32, (pages, came), 1)
    came_page = lax.shift_right_logical(came_row, page_rows.bit_length() - 1)
    came_slot = lax.broadcasted_iota(jnp.int32, (pages, came), 0) * page_rows
    came_slot = came_slot + came_row - came_page * page_rows
    uses = (page_col == came_page + pool_pages) & (came_slot < length)
    uses = jnp.sum(jnp.where(uses, 1.0, 0.0), axis=0, keepdims=True)

    swap_rows.wait()
    summed = own_v[...] + got_v[...].astype(jnp.float32)
    own_v[...] = summed
    stat_v[...] = jnp.broadcast_to(jnp.sum(summed * summed, axis=-1, keepdims=True), stat_v.shape)
    swap_stat = swap(stat_v, gstat_v, 1)

    queries = qv_v[...]
    old = jnp.where(here > 0.0, dot_t(queries, cached[:, :HEAD]), neg_large)
    new = dot_t(queries, kv_v[rows:, :HEAD])
    step = jnp.bitwise_and(lax.broadcasted_iota(jnp.int32, new.shape, 0), PAD - 1)
    new = jnp.where(lax.broadcasted_iota(jnp.int32, new.shape, 1) <= step, new, neg_large)
    peak = jnp.maximum(
        jnp.max(old, axis=-1, keepdims=True), jnp.max(new, axis=-1, keepdims=True)
    )
    old = jnp.exp(old - peak)
    new = jnp.exp(new - peak)
    total = jnp.sum(old, axis=-1, keepdims=True) + jnp.sum(new, axis=-1, keepdims=True)
    mixed = dot(old.astype(jnp.bfloat16), cached[:, HEAD:])
    mixed = mixed + dot(new.astype(jnp.bfloat16), kv_v[rows:, HEAD:])

    got_pgain.wait()
    gain = pgain_v[:, pl.ds(mine, half)]
    swap_stat.wait()
    square = stat_v[:, 0:1] + gstat_v[:, 0:1]
    scale = lax.rsqrt(square / width + eps_norm)
    out_v[...] = (
        x_v[:, pl.ds(mine, half)].astype(jnp.float32) + own_v[...] * scale * gain
    ).astype(out_v.dtype)
    put_out = put(out_v, prefill_out)

    def arrive(step, carry):
        s = lax.rem(me + n - step, n)
        pltpu.make_async_remote_copy(
            src_ref=leaving.at[s],
            dst_ref=arrived.at[s],
            send_sem=page_send.at[s],
            recv_sem=page_recv.at[s],
            device_id=(s, side),
            device_id_type=MESH,
        ).wait()
        return carry

    lax.fori_loop(1, n, arrive, 0)


    moved = arrived[...].reshape(came, 2 * HEAD)
    scores = jnp.where(uses > 0.0, dot_t(queries, moved[:, :HEAD]), neg_large)
    top = jnp.maximum(peak, jnp.max(scores, axis=-1, keepdims=True))
    weights = uses * jnp.exp(scores - top)
    keep = jnp.exp(peak - top)
    total = total * keep + jnp.sum(weights, axis=-1, keepdims=True)
    mixed = mixed * keep + dot(weights.astype(jnp.bfloat16), moved[:, HEAD:])
    mixed = (mixed * (1.0 / total)).astype(jnp.bfloat16)
    for i in range(heads):
        vattn_v[:, i * HEAD:(i + 1) * HEAD] = mixed[i * PAD:(i + 1) * PAD, :]

    vsend_v[0] = dot(vattn_v[...], wo_v[0])
    vsend_v[1] = dot(vattn_v[...], wo_v[1])
    swap_verify = swap(vsend_v, vgot_v, 2)

    swap_verify.wait()
    ours = vsend_v[1] + vgot_v[0]
    other = vsend_v[0] + vgot_v[1]
    square = jnp.sum(ours * ours, axis=-1, keepdims=True)
    square = square + jnp.sum(other * other, axis=-1, keepdims=True)
    final = vx_v[:, pl.ds(mine, half)] + ours * lax.rsqrt(square / width + eps_norm) * gain
    vout_v[0] = final[0:draft, :].astype(vout_v.dtype)
    put_vout = put(vout_v, verify_out)
    for copy in (put_kv, put_vkv, put_out, put_vout):
        copy.wait()


def write_out(count, *refs):
    sources, results, held = refs[:count], refs[count:2 * count], refs[2 * count:3 * count]
    in_sem, out_sem = refs[3 * count:]
    ins = [pltpu.make_async_copy(sources[k], held[k], in_sem.at[k]) for k in range(count)]
    outs = [pltpu.make_async_copy(held[k], results[k], out_sem.at[k]) for k in range(count)]
    for copy in ins:
        copy.start()
    for k in range(count):
        ins[k].wait()
        outs[k].start()
    for copy in outs:
        copy.wait()


def on_device(
    verify_x, prefill_x, attn_gain, w_query, w_keyval, qk_gain, w_out, post_gain,
    page_pool, outbound, page_table, cache_len, prompt_len, accepted,
):
    n = lax.axis_size("req")
    _, draft, width = verify_x.shape
    rows = prefill_x.shape[0]
    all_rows = rows + PAD
    columns = w_query.shape[1]
    heads = columns // HEAD
    half = width // 2
    pages = page_table.shape[1]
    page = page_pool.shape[1:]
    table, high = rope_tables(pages * page[0] + draft)
    bf16, f32 = jnp.bfloat16, jnp.float32
    hbm = pl.BlockSpec(memory_space=pltpu.HBM)
    moved = 22 + heads
    results = pl.pallas_call(
        functools.partial(kernel, n),
        out_shape=(
            jax.ShapeDtypeStruct((1, draft, half), bf16),
            jax.ShapeDtypeStruct((rows, half), bf16),
            jax.ShapeDtypeStruct((1, draft, 2 * HEAD), bf16),
            jax.ShapeDtypeStruct((rows, 2 * HEAD), bf16),
        ),
        in_specs=[hbm] * 16,
        out_specs=(hbm,) * 4,
        scratch_shapes=[
            pltpu.SMEM(outbound.shape, jnp.int32),
            pltpu.SMEM(page_table.shape, jnp.int32),
            pltpu.SMEM((1, 1), jnp.int32),
            pltpu.SMEM(prompt_len.shape, jnp.int32),
            pltpu.SMEM((1, 1), jnp.int32),
            pltpu.VMEM(verify_x.shape, bf16),
            pltpu.VMEM(page_table.shape, jnp.int32),
            pltpu.VMEM((rows, width), bf16),
            pltpu.VMEM((PAD, width), f32),
            pltpu.VMEM((1, width), f32),
            pltpu.VMEM((1, width), f32),
            pltpu.VMEM(qk_gain.shape, f32),
            pltpu.VMEM(table.shape, bf16),
            pltpu.VMEM(high.shape, f32),
            pltpu.VMEM((2 + heads, width, HEAD), bf16),
            pltpu.VMEM((2, columns, half), bf16),
            pltpu.VMEM(page_pool.shape, bf16),
            pltpu.VMEM((n,) + page, bf16),
            pltpu.VMEM((n,) + page, bf16),
            pltpu.VMEM((pages * page[0], page[1]), bf16),
            pltpu.VMEM((all_rows, width), bf16),
            pltpu.VMEM((all_rows, HALF), f32),
            pltpu.VMEM((all_rows, HALF), f32),
            pltpu.VMEM((rows, rows), f32),
            pltpu.VMEM((all_rows, 2 * HEAD), bf16),
            pltpu.VMEM((heads * PAD, HEAD), bf16),
            pltpu.VMEM((rows, columns), bf16),
            pltpu.VMEM((PAD, columns), bf16),
            pltpu.VMEM((rows, half), f32),
            pltpu.VMEM((rows, half), bf16),
            pltpu.VMEM((rows, half), bf16),
            pltpu.VMEM((rows, 128), f32),
            pltpu.VMEM((rows, 128), f32),
            pltpu.VMEM((2, PAD, half), f32),
            pltpu.VMEM((2, PAD, half), f32),
            pltpu.VMEM((rows, half), bf16),
            pltpu.VMEM((1, draft, half), bf16),
            pltpu.VMEM((1, draft, 2 * HEAD), bf16),
            pltpu.SemaphoreType.DMA((moved,)),
            pltpu.SemaphoreType.DMA((n,)),
            pltpu.SemaphoreType.DMA((n,)),
            pltpu.SemaphoreType.DMA((3,)),
            pltpu.SemaphoreType.DMA((3,)),
        ],
        compiler_params=pltpu.CompilerParams(
            collective_id=0, has_side_effects=True, vmem_limit_bytes=VMEM_LIMIT
        ),
        cost_estimate=pl.CostEstimate(
            flops=2 * all_rows * width * (2 * columns + 2 * HEAD),
            bytes_accessed=16 * 1024 * 1024,
            transcendentals=heads * rows * rows,
        ),
    )(
        outbound, page_table, cache_len[None], prompt_len, accepted[None],
        verify_x, prefill_x, attn_gain.reshape(1, -1), w_query, w_keyval, qk_gain, w_out,
        post_gain.reshape(1, -1), page_pool, jnp.asarray(table), jnp.asarray(high),
    )
    return pl.pallas_call(
        functools.partial(write_out, len(results)),
        out_shape=tuple(jax.ShapeDtypeStruct(r.shape, r.dtype) for r in results),
        in_specs=[pl.BlockSpec(memory_space=pl.ANY)] * 4,
        out_specs=(hbm,) * 4,
        scratch_shapes=[pltpu.VMEM(r.shape, r.dtype) for r in results]
        + [pltpu.SemaphoreType.DMA((len(results),))] * 2,
        compiler_params=pltpu.CompilerParams(vmem_limit_bytes=VMEM_LIMIT),
    )(*results)


def solution(mesh):
    placed = (
        P("req", None, None),
        P("req", None),
        P(),
        P(None, "head"),
        P(None, "head"),
        P(),
        P("head", None),
        P(),
        P("req", None, "head"),
        P("req", None),
        P("req", None),
        P("req"),
        P("req", None),
        P("req"),
    )
    return jax.shard_map(
        on_device,
        mesh=mesh,
        in_specs=placed,
        out_specs=(
            P("req", None, "head"),
            P("req", "head"),
            P("req", None, "head"),
            P("req", "head"),
        ),
        check_vma=False,
    )
```
